32 devices in a mesh: xb: 8 (over z, y), yb: 4 (over x, core).
Axes of the slice: x: 2, y: 2, z: 4, core: 2. Of those that a mesh axis runs over, the one named last changes fastest.
Arguments:
- initial_guess: float32 [64, 256, 256], P('xb', 'yb'), may hold values from -4 to 4
- right_side: float32 [64, 256, 256], P('xb', 'yb'), may hold values from -8 to 8
- coefficient: float32 [64, 256, 256], P('xb', 'yb'), may hold values from 0.3 to 3
Outputs:
- fine_field: float32 [64, 256, 256], P('xb', 'yb')
- middle_field: float32 [32, 128, 128], P('xb', 'yb')
- lower_field: float32 [16, 64, 64], P('xb', 'yb')
- coarse_field: float32 [8, 32, 32], P('xb', 'yb')
The draws below stay inside these ranges and needn't reach their ends.
All inputs are finite; a program needn't handle non-finite values.
Results may differ from the reference program's by a relative error of at most 0.00002.
Values sent between devices are 32-bit elements; how exact they have to be, the bound alone decides.
A program may use at most 192 MiB of HBM per device.

```python
import math
import jax
import jax.numpy as jnp

COARSE_ITERS = 8
NX = 64
NY = 256
NZ = 256


def block_levels(stream_key, dims, cuts, low, high):
    factor_of = 1.0
    for dim, blocks in cuts:
        draws = jax.random.uniform(jax.random.fold_in(jax.random.fold_in(stream_key, 6), dim), (blocks,), jnp.float32, low / len(cuts), high / len(cuts))
        factor_of = factor_of * jnp.repeat(jnp.exp(draws), dims[dim] // blocks).reshape((-1,) + (1,) * (len(dims) - 1 - dim))
    return factor_of


def scatter_about(own_key, extent, spread, bound, split=(), held_as=jnp.bfloat16):
    drawn = jax.random.normal(own_key, extent, jnp.float32) * spread
    if len(split) > 0:
        drawn = block_levels(own_key, extent, split, -0.22, 0.18) * drawn
    return jnp.clip(drawn, min=-bound, max=bound).astype(held_as)


def setup_inputs(seed: int = 0) -> dict:
    arg_keys = jax.random.split(jax.random.key(seed), 4)
    return {
        "initial_guess": scatter_about(arg_keys[0], (NX, NY, NZ), 0.5, 4.0, ((0, 8), (1, 4)), jnp.float32),
        "right_side": scatter_about(arg_keys[1], (NX, NY, NZ), 1.0, 8.0, ((0, 8), (1, 4)), jnp.float32),
        "coefficient": jnp.clip(jnp.exp(math.log(3.0) - 2.3025851 * jax.random.uniform(arg_keys[2], (NX, NY, NZ), jnp.float32) ** block_levels(arg_keys[2], (NX, NY, NZ), ((0, 8), (1, 4)), -0.2, 0.2)), 0.3, 3.0),
    }


damping_alpha = 0.05
cheb_theta = 1.15
cheb_delta = 0.85
cheb_sigma = cheb_theta / cheb_delta
cheb_first = 1.0 / cheb_sigma
cheb_second = 1.0 / (2.0 * cheb_sigma - cheb_first)
cheb_carry = cheb_second * cheb_first
cheb_resid = 2.0 * cheb_second / cheb_delta
jacobi_weight = 0.8


def neighbours(padded):
    return [padded[2:, 1:-1, 1:-1], padded[:-2, 1:-1, 1:-1], padded[1:-1, 2:, 1:-1],
            padded[1:-1, :-2, 1:-1], padded[1:-1, 1:-1, 2:], padded[1:-1, 1:-1, :-2]]


def face_weights(padded_coef, scale):
    centre = padded_coef[1:-1, 1:-1, 1:-1]
    weights = [(0.5 * scale) * (centre + other) for other in neighbours(padded_coef)]
    diagonal = damping_alpha + weights[0]
    for other in weights[1:]:
        diagonal = diagonal + other
    return weights, diagonal


def apply_operator(padded, field, weights, diagonal):
    result = diagonal * field
    for weight, other in zip(weights, neighbours(padded)):
        result = result - weight * other
    return result


def smooth_level(start, right_side, coefficient, scale, extend):
    weights, diagonal = face_weights(extend(coefficient), scale)
    if start is None:
        start = jnp.zeros_like(right_side)
        residual = right_side
    else:
        residual = right_side - apply_operator(extend(start), start, weights, diagonal)
    first_step = residual / (cheb_theta * diagonal)
    first = start + first_step
    residual = right_side - apply_operator(extend(first), first, weights, diagonal)
    second_step = cheb_carry * first_step + cheb_resid * residual / diagonal
    second = first + second_step
    residual = right_side - apply_operator(extend(second), second, weights, diagonal)
    return second, residual


def restrict_field(field):
    sx, sy, sz = field.shape
    return field.reshape(sx // 2, 2, sy // 2, 2, sz // 2, 2).sum(axis=(1, 3, 5)) * 0.125


def coarse_solve(right_side, coefficient, scale, extend):
    weights, diagonal = face_weights(extend(coefficient), scale)
    field = jnp.zeros_like(right_side)
    for repeat in range(COARSE_ITERS):
        field = field + jacobi_weight * (right_side - apply_operator(extend(field), field, weights, diagonal)) / diagonal
    leftover = right_side - apply_operator(extend(field), field, weights, diagonal)
    ones_field = jnp.ones_like(right_side)
    image_ones = apply_operator(extend(ones_field), ones_field, weights, diagonal)
    return field + jnp.sum(leftover) / jnp.sum(image_ones)


def extend_all(field):
    return jnp.pad(field, 1)


def reference(initial_guess, right_side, coefficient):
    fine, fine_res = smooth_level(initial_guess, right_side, coefficient, 1.0, extend_all)
    mid_coef = restrict_field(coefficient)
    middle, mid_res = smooth_level(None, restrict_field(fine_res), mid_coef, 0.25, extend_all)
    low_coef = restrict_field(mid_coef)
    lower, low_res = smooth_level(None, restrict_field(mid_res), low_coef, 0.0625, extend_all)
    coarse = coarse_solve(restrict_field(low_res), restrict_field(low_coef), 0.015625, extend_all)
    return fine, middle, lower, coarse
```

```python
import functools

import jax
import jax.numpy as jnp
from jax import lax
from jax.experimental import pallas as pl
from jax.experimental.pallas import tpu as pltpu
from jax.sharding import PartitionSpec as P

COARSE_ITERS = 8
MESH = pl.DeviceIdType.MESH

damping_alpha = 0.05
cheb_theta = 1.15
cheb_delta = 0.85
cheb_sigma = cheb_theta / cheb_delta
cheb_first = 1.0 / cheb_sigma
cheb_second = 1.0 / (2.0 * cheb_sigma - cheb_first)
cheb_carry = cheb_second * cheb_first
cheb_resid = 2.0 * cheb_second / cheb_delta
jacobi_weight = 0.8

K0, V0, E0, G0, K1, E1, G1, K2, E2 = range(9)


def lane_of(shape):
    return lax.broadcasted_iota(jnp.int32, shape, 1)


def row_of(shape):
    return lax.broadcasted_iota(jnp.int32, shape, 0)


def pair_matrix(rows, columns, valid, offset=0):
    source = row_of((rows, columns))
    target = lane_of((rows, columns)) - offset
    hit = (source // 2 == target) & (source < valid) & (target >= 0)
    return hit.astype(jnp.float32)


def fold_lanes(value, matrix):
    return jnp.dot(
        value, matrix, precision=lax.Precision.HIGHEST, preferred_element_type=jnp.float32
    )


def pair_rows(value, fold):
    n = value.shape[0]
    parts = []
    for t in range(value.shape[1] // 128):
        fold[t, 0:n, :] = value[:, 128 * t : 128 * (t + 1)]
        parts.append(
            fold[t, pl.ds(0, n // 2, stride=2), :] + fold[t, pl.ds(1, n // 2, stride=2), :]
        )
    return parts[0] if len(parts) == 1 else jnp.concatenate(parts, axis=1)


class Level:
    def __init__(self, dims, valid, scale, refs):
        self.nx, self.ny, self.lanes = dims
        self.valid = valid
        self.c = 0.5 * scale
        self.wx, self.wy, self.wl, self.wz, self.al, self.di = refs

    def inner_faces(self, k):
        shape = (self.ny, self.lanes)
        lane = lane_of(shape)
        for i in range(self.nx):
            own = k(i)
            if i + 1 < self.nx:
                self.wx[i + 1] = self.c * (own + k(i + 1))
            wz = self.c * (own + pltpu.roll(own, self.lanes - 1, 1))
            self.wz[i] = jnp.where(lane < self.valid - 1, wz, 0.0)
            edge = (lane == 0) | (lane == self.valid - 1)
            self.al[i] = damping_alpha + jnp.where(edge, self.c * own, 0.0)

    def y_faces(self, k, ky):
        shape = (self.ny, self.lanes)
        row = row_of(shape)
        for i in range(self.nx):
            own = k(i)
            up = jnp.where(row == self.ny - 1, ky[1, i : i + 1, :], pltpu.roll(own, self.ny - 1, 0))
            self.wy[i] = self.c * (own + up)
            self.wl[i : i + 1, :] = self.c * (own[0:1] + ky[0, i : i + 1, :])

    def x_faces(self, k, kx):
        self.wx[0] = self.c * (k(0) + kx[0])
        self.wx[self.nx] = self.c * (k(self.nx - 1) + kx[1])

    def diagonal(self, i):
        wz, wy = self.wz[i], self.wy[i]
        row = row_of((self.ny, self.lanes))
        below = jnp.where(row == 0, self.wl[i : i + 1, :], pltpu.roll(wy, 1, 0))
        total = self.al[i] + (wz + pltpu.roll(wz, 1, 1)) + (wy + below)
        self.di[i] = 1.0 / (total + (self.wx[i] + self.wx[i + 1]))

    def operate(self, i, v, vx, vy):
        shape = (self.ny, self.lanes)
        row = row_of(shape)
        own = v(i)
        fz = self.wz[i] * (own - pltpu.roll(own, self.lanes - 1, 1))
        result = self.al[i] * own + (fz - pltpu.roll(fz, 1, 1))
        over = vy[1, i : i + 1, :] if vy is not None else 0.0
        up = jnp.where(row == self.ny - 1, over, pltpu.roll(own, self.ny - 1, 0))
        fy = self.wy[i] * (own - up)
        low = self.wl[i : i + 1, :] * ((vy[0, i : i + 1, :] if vy is not None else 0.0) - own[0:1])
        result = result + (fy - jnp.where(row == 0, low, pltpu.roll(fy, 1, 0)))
        for face, j, side in ((i, i - 1, 0), (i + 1, i + 1, 1)):
            if 0 <= j < self.nx:
                result = result + self.wx[face] * (own - v(j))
            elif vx is not None:
                result = result + self.wx[face] * (own - vx[side])
            else:
                result = result + self.wx[face] * own
        return result


def kernel(nxb, nyb, v0_ref, f_ref, k_ref, fine, middle, lower, coarse, *scratch):
    names = []
    for l in range(3):
        fields = ("d0", "v1") if l == 0 else ("f%d" % l, "k%d" % l, "d%d" % l, "v2%d" % l)
        names += [*fields, *("%s%d" % (n, l) for n in ("wx", "wy", "wl", "wz", "al", "di", "fold"))]
    names += ["gx0", "gx1", "part", "kpart", "part_in", "kpart_in", "mine", "kmine"]
    names += ["whole", "kwhole", "last"]
    names += ["%s%d" % (n, e) for n in ("hx", "hy", "py") for e in range(9)]
    names += ["send", "recv", "psend", "precv", "kpsend", "kprecv"]
    names += ["wsend", "wrecv", "kwsend", "kwrecv"]
    s = dict(zip(names, scratch, strict=True))
    hx = [s["hx%d" % e] for e in range(9)]
    hy = [s["hy%d" % e] for e in range(9)]
    py = [s["py%d" % e] for e in range(9)]
    xi, yj = lax.axis_index("xb"), lax.axis_index("yb")
    has = (xi > 0, xi < nxb - 1, yj > 0, yj < nyb - 1)
    beside = (
        (jnp.maximum(xi - 1, 0), yj),
        (jnp.minimum(xi + 1, nxb - 1), yj),
        (xi, jnp.maximum(yj - 1, 0)),
        (xi, jnp.minimum(yj + 1, nyb - 1)),
    )

    barrier = pltpu.get_barrier_semaphore()

    def greet(device):
        pl.semaphore_signal(barrier, inc=1, device_id=device, device_id_type=MESH)

    for o in range(1, nyb):
        greet((xi, lax.rem(yj + o, nyb)))
    for side in (0, 1):
        @pl.when(has[side])
        def _():
            for y in range(nyb):
                greet((beside[side][0], jnp.int32(y)))
    for o in range(1, nxb):
        x = lax.rem(xi + o, nxb)

        @pl.when((x - xi > 1) | (xi - x > 1))
        def _():
            greet((x, yj))
    rows = has[0].astype(jnp.int32) + has[1].astype(jnp.int32)
    pl.semaphore_wait(barrier, (nyb - 1) + nyb * rows + (nxb - 1 - rows))

    def copy(e, side, src):
        dst = (hx if side < 2 else hy)[e].at[1 - side % 2]
        return pltpu.make_async_remote_copy(
            src_ref=src,
            dst_ref=dst,
            send_sem=s["send"].at[e, side],
            recv_sem=s["recv"].at[e, side],
            device_id=beside[side],
            device_id_type=MESH,
        )

    started = []

    def put(e, side, src):
        made = copy(e, side, src)
        pl.when(has[side])(made.start)
        started.append((made, side))
        away = (hx if side < 2 else hy)[e]

        @pl.when(jnp.logical_not(has[side]))
        def _():
            away[side % 2] = jnp.zeros(away.shape[1:], jnp.float32)

    def get(e, sides):
        for side in sides:
            other = side ^ 1
            buffer = (hx if side < 2 else hy)[e]
            made = pltpu.make_async_remote_copy(
                src_ref=buffer.at[side % 2],
                dst_ref=buffer.at[side % 2],
                send_sem=s["send"].at[e, other],
                recv_sem=s["recv"].at[e, other],
                device_id=beside[other],
                device_id_type=MESH,
            )
            pl.when(has[side])(made.wait_recv)

    def put_x(e, ref):
        put(e, 0, ref.at[0])
        put(e, 1, ref.at[ref.shape[0] - 1])

    def pack(e, i, value):
        n = value.shape[0]
        py[e][0, i : i + 1, :] = value[0:1]
        py[e][1, i : i + 1, :] = value[n - 1 : n]

    def put_y(e):
        put(e, 2, py[e].at[0])
        put(e, 3, py[e].at[1])

    def restrict(planes, matrix, fold, out):
        n = planes[0].shape[0]
        pairs = [planes[2 * i] + planes[2 * i + 1] for i in range(len(planes) // 2)]
        folded = fold_lanes(jnp.concatenate(pairs, axis=0), matrix) * 0.125
        summed = pair_rows(folded, fold)
        for i in range(len(pairs)):
            out[i] = summed[i * (n // 2) : (i + 1) * (n // 2)]

    def gather_rows(src, into, send, recv, offsets):
        made = []
        for t, step in enumerate(offsets):
            for o in range(nyb):
                if step == 0 and o == 0:
                    continue
                y = lax.rem(yj + o, nyb)
                side = 0 if step < 0 else 1
                x = xi if step == 0 else beside[side][0]
                one = pltpu.make_async_remote_copy(
                    src_ref=src.at[t],
                    dst_ref=into.at[t, yj],
                    send_sem=send.at[t, o],
                    recv_sem=recv.at[t, yj],
                    device_id=(x, y),
                    device_id_type=MESH,
                )
                if step == 0:
                    one.start()
                else:
                    pl.when(has[side])(one.start)
                made.append((one, step))
        return made

    def gathered_rows(src, into, send, recv, offsets):
        total = src[offsets.index(0)]
        for t, step in enumerate(offsets):
            for o in range(nyb):
                if step == 0 and o == 0:
                    continue
                y = lax.rem(yj + o, nyb)
                side = 1 if step < 0 else 0
                one = pltpu.make_async_remote_copy(
                    src_ref=into.at[t, y],
                    dst_ref=into.at[t, y],
                    send_sem=send.at[t, o],
                    recv_sem=recv.at[t, y],
                    device_id=(xi, lax.rem(yj + 1, nyb)),
                    device_id_type=MESH,
                )
                if step == 0:
                    one.wait_recv()
                else:
                    pl.when(has[side])(one.wait_recv)

                    @pl.when(jnp.logical_not(has[side]))
                    def _():
                        into[t, y] = jnp.zeros(into.shape[2:], jnp.float32)
                total = total + into[t, y]
        return total

    def gather_columns(src, into, send, recv):
        made = []
        for o in range(1, nxb):
            one = pltpu.make_async_remote_copy(
                src_ref=src,
                dst_ref=into.at[xi],
                send_sem=send.at[o],
                recv_sem=recv.at[xi],
                device_id=(lax.rem(xi + o, nxb), yj),
                device_id_type=MESH,
            )
            one.start()
            made.append(one)
        return made

    def gathered_columns(src, into, send, recv):
        into[xi] = src[...]
        for o in range(1, nxb):
            x = lax.rem(xi + o, nxb)
            pltpu.make_async_remote_copy(
                src_ref=into.at[x],
                dst_ref=into.at[x],
                send_sem=send.at[o],
                recv_sem=recv.at[x],
                device_id=(lax.rem(xi + 1, nxb), yj),
                device_id_type=MESH,
            ).wait_recv()

    nx, ny, nz = k_ref.shape
    levels = []
    for l in range(3):
        dims = (nx >> l, ny >> l, max(nz >> l, 128))
        refs = [s["%s%d" % (n, l)] for n in ("wx", "wy", "wl", "wz", "al", "di")]
        levels.append(Level(dims, nz >> l, 0.25**l, refs))
    low3, nz3 = ny // 8, nz // 8
    wide = nyb * nz3
    s01 = pair_matrix(nz, max(nz // 2, 128), nz)
    s12 = pair_matrix(max(nz // 2, 128), max(nz // 4, 128), nz // 2)

    def s23(offset):
        return pair_matrix(max(nz // 4, 128), wide, nz // 4, offset * nz3)

    put_x(K0, k_ref)
    put_x(V0, v0_ref)
    for i in range(nx):
        pack(K0, i, k_ref[i])
        pack(V0, i, v0_ref[i])
    put_y(K0)
    put_y(V0)

    restrict([k_ref[i] for i in range(nx)], s01, s["fold0"], s["k1"])
    put_x(K1, s["k1"])
    for i in range(nx // 2):
        pack(K1, i, s["k1"][i])
    put_y(K1)
    restrict([s["k1"][i] for i in range(nx // 2)], s12, s["fold1"], s["k2"])
    put_x(K2, s["k2"])
    for i in range(nx // 4):
        pack(K2, i, s["k2"][i])
    put_y(K2)
    restrict([s["k2"][i] for i in range(nx // 4)], s23(yj), s["fold2"], s["kpart"])
    kargs = (s["kpart"], s["kpart_in"], s["kpsend"], s["kprecv"], (0,))
    krows = gather_rows(*kargs)

    top = levels[0]
    inner, outer = list(range(1, nx - 1)), [0, nx - 1]
    k = lambda i: k_ref[i]
    v0 = lambda i: v0_ref[i]
    d0, v1 = s["d0"], s["v1"]
    top.inner_faces(k)
    get(K0, (2, 3))
    get(V0, (2, 3))
    top.y_faces(k, hy[K0])

    def first(i):
        top.diagonal(i)
        r = f_ref[i] - top.operate(i, v0, hx[V0], hy[V0])
        d = r * (top.di[i] * (1.0 / cheb_theta))
        d0[i] = d
        v = v0_ref[i] + d
        v1[i] = v
        pack(E0, i, v)

    for i in inner:
        first(i)
    get(K0, (0, 1))
    get(V0, (0, 1))
    top.x_faces(k, hx[K0])
    for i in outer:
        first(i)
    put_x(E0, v1)
    put_y(E0)

    s["kmine"][...] = gathered_rows(*kargs)
    kcargs = (s["kmine"], s["kwhole"], s["kwsend"], s["kwrecv"])
    kcolumns = gather_columns(*kcargs)
    for l, e, ref in ((1, K1, s["k1"]), (2, K2, s["k2"])):
        level = levels[l]
        kl = functools.partial(lambda ref, i: ref[i], ref)
        level.inner_faces(kl)
        get(e, (0, 1, 2, 3))
        level.y_faces(kl, hy[e])
        level.x_faces(kl, hx[e])
        for i in range(level.nx):
            level.diagonal(i)

    get(E0, (2, 3))

    def second(level, i, f, v1, d0, e, out):
        r = f(i) - level.operate(i, v1, hx[e], hy[e])
        v = v1(i) + (cheb_carry * d0(i) + (cheb_resid * level.di[i]) * r)
        out[i] = v
        return v

    f0 = lambda i: f_ref[i]
    v1at = lambda i: v1[i]
    d0at = lambda i: d0[i]
    for i in inner:
        second(top, i, f0, v1at, d0at, E0, fine)
    get(E0, (0, 1))
    for i in outer:
        second(top, i, f0, v1at, d0at, E0, fine)

    def face_sums(level, out, matrix, e, gx, fold):
        n = level.ny
        both = [level.wx[0] * out[0], level.wx[level.nx] * out[level.nx - 1]]
        folded = fold_lanes(jnp.concatenate(both, axis=0), matrix) * 0.125
        summed = pair_rows(folded, fold)
        for side in (0, 1):
            gx[side] = summed[side * (n // 2) : (side + 1) * (n // 2)]
        put_x(e, gx)
        lows, highs = [], []
        for i in range(level.nx // 2):
            a, b = 2 * i, 2 * i + 1
            lows.append(level.wl[a : a + 1, :] * out[a, 0:1, :] + level.wl[b : b + 1, :] * out[b, 0:1, :])
            highs.append(
                level.wy[a, n - 1 : n, :] * out[a, n - 1 : n, :]
                + level.wy[b, n - 1 : n, :] * out[b, n - 1 : n, :]
            )
        m = level.nx // 2
        pad = [jnp.zeros((8 - m, level.lanes), jnp.float32)]
        tops = [jnp.concatenate(part + pad, axis=0) for part in (lows, highs)]
        folded = fold_lanes(jnp.concatenate(tops, axis=0), matrix) * 0.125
        py[e][0] = folded[0:m]
        py[e][1] = folded[8 : 8 + m]
        put_y(e)

    def next_side(level, f, out, matrix, e, gx, fold, into):
        at = lambda i: out[i]
        face_sums(level, out, matrix, e, gx, fold)
        left = [f(i) - level.operate(i, at, None, None) for i in range(level.nx)]
        restrict(left, matrix, fold, into)
        get(e, (0, 1, 2, 3))
        m, n = level.nx // 2, level.ny // 2
        row = row_of((n, into.shape[2]))
        for i in range(m):
            value = into[i]
            if i == 0:
                value = value + hx[e][0]
            if i == m - 1:
                value = value + hx[e][1]
            value = value + jnp.where(row == 0, hy[e][0, i : i + 1, :], 0.0)
            into[i] = value + jnp.where(row == n - 1, hy[e][1, i : i + 1, :], 0.0)

    next_side(top, f0, fine, s01, G0, s["gx0"], s["fold0"], s["f1"])

    def correct(level, f, d, e, out):
        for i in range(level.nx):
            value = f[i] * (level.di[i] * (1.0 / cheb_theta))
            d[i] = value
            pack(e, i, value)
        put_x(e, d)
        put_y(e)
        get(e, (0, 1, 2, 3))
        at = lambda i: d[i]
        for i in range(level.nx):
            second(level, i, lambda i: f[i], at, at, e, out)

    correct(levels[1], s["f1"], s["d1"], E1, s["v21"])
    next_side(levels[1], lambda i: s["f1"][i], s["v21"], s12, G1, s["gx1"], s["fold1"], s["f2"])
    middle[...] = s["v21"][:, :, 0 : nz // 2]
    low = levels[2]
    correct(low, s["f2"], s["d2"], E2, s["v22"])

    v2, f2, part = s["v22"], s["f2"], s["part"]
    n = low.ny
    left = f2[0] - low.operate(0, lambda i: v2[i], None, None)
    left = left + (f2[1] - low.operate(1, lambda i: v2[i], None, None))
    stack = [left, low.wx[0] * v2[0], low.wx[2] * v2[1]]
    folded = fold_lanes(jnp.concatenate(stack, axis=0), s23(yj)) * 0.125
    summed = pair_rows(folded, s["fold2"])
    tiles = [summed[t * (n // 2) : (t + 1) * (n // 2)] for t in range(3)]
    down = low.wl[0:1, :] * v2[0, 0:1, :] + low.wl[1:2, :] * v2[1, 0:1, :]
    up = low.wy[0, n - 1 : n, :] * v2[0, n - 1 : n, :] + low.wy[1, n - 1 : n, :] * v2[1, n - 1 : n, :]
    eight = (8, low.lanes)
    down = fold_lanes(jnp.broadcast_to(down, eight), s23(yj - 1)) * 0.125
    up = fold_lanes(jnp.broadcast_to(up, eight), s23(yj + 1)) * 0.125
    row = row_of((low3, wide))
    own = tiles[0] + jnp.where(row == low3 - 1, down[0:1], 0.0) + jnp.where(row == 0, up[0:1], 0.0)
    part[0] = tiles[1]
    part[1] = own
    part[2] = tiles[2]
    fargs = (part, s["part_in"], s["psend"], s["precv"], (-1, 0, 1))
    frows = gather_rows(*fargs)
    lower[...] = v2[:, :, 0 : nz // 4]

    gathered_columns(*kcargs)
    shape = (nxb, wide)
    lane, xrow = lane_of(shape), row_of(shape)
    z = lax.rem(lane, nz3)
    inside = (xrow > 0, xrow < nxb - 1, z > 0, z < nz3 - 1)
    below = lane >= nz3
    above = lane < wide - nz3
    c = 0.5 * 0.25**3

    def around(v):
        first = jnp.where(below, pltpu.roll(v[-1], nz3, 1), 0.0)
        final = jnp.where(above, pltpu.roll(v[0], wide - nz3, 1), 0.0)
        out = []
        for r in range(low3):
            own = v[r]
            out.append(
                (
                    jnp.where(inside[0], pltpu.roll(own, 1, 0), 0.0),
                    jnp.where(inside[1], pltpu.roll(own, nxb - 1, 0), 0.0),
                    jnp.where(inside[2], pltpu.roll(own, 1, 1), 0.0),
                    jnp.where(inside[3], pltpu.roll(own, wide - 1, 1), 0.0),
                    v[r - 1] if r > 0 else first,
                    v[r + 1] if r < low3 - 1 else final,
                )
            )
        return out

    kc = [s["kwhole"][:, r, :] for r in range(low3)]
    weights = [[c * (kc[r] + other) for other in near] for r, near in enumerate(around(kc))]
    diagonal = [damping_alpha + sum(w) for w in weights]
    step = [jacobi_weight / d for d in diagonal]

    def operate(v):
        return [
            diagonal[r] * v[r] - sum(w * other for w, other in zip(weights[r], near))
            for r, near in enumerate(around(v))
        ]

    image = sum(operate([jnp.ones(shape, jnp.float32)] * low3))
    s["mine"][...] = gathered_rows(*fargs)
    fcargs = (s["mine"], s["whole"], s["wsend"], s["wrecv"])
    fcolumns = gather_columns(*fcargs)
    image = jnp.sum(image)
    gathered_columns(*fcargs)
    fc = [s["whole"][:, r, :] for r in range(low3)]
    v = [step[r] * fc[r] for r in range(low3)]
    for _ in range(COARSE_ITERS - 1):
        image_v = operate(v)
        v = [v[r] + step[r] * (fc[r] - image_v[r]) for r in range(low3)]
    image_v = operate(v)
    shift = jnp.sum(sum(fc[r] - image_v[r] for r in range(low3))) / image
    for r in range(low3):
        s["last"][:, r, :] = v[r] + shift
    block = s["last"][xi]
    coarse[0] = pltpu.roll(block, lax.rem(wide - yj * nz3, wide), 1)[:, 0:nz3]

    for made, side in started:
        pl.when(has[side])(made.wait_send)
    for made, step_x in krows + frows:
        if step_x == 0:
            made.wait_send()
        else:
            pl.when(has[0 if step_x < 0 else 1])(made.wait_send)
    for made in kcolumns + fcolumns:
        made.wait_send()


def per_device(nxb, nyb, initial_guess, right_side, coefficient):
    nx, ny, nz = coefficient.shape
    vm = lambda *shape: pltpu.VMEM(shape, jnp.float32)
    dma = lambda *shape: pltpu.SemaphoreType.DMA(shape)
    dims = [(nx >> l, ny >> l, max(nz >> l, 128)) for l in range(3)]
    low3, nz3 = ny // 8, nz // 8
    wide = nyb * nz3
    scratch = []
    for l, (a, b, c) in enumerate(dims):
        if l == 0:
            scratch += [vm(a, b, c), vm(a, b, c)]
        else:
            scratch += [vm(a, b, c)] * 4
        scratch += [vm(a + 1, b, c), vm(a, b, c), vm(a, c), vm(a, b, c), vm(a, b, c), vm(a, b, c)]
        folded = dims[l + 1][2] if l < 2 else wide
        scratch += [vm(folded // 128, max(a // 2, 3) * b + 8, 128)]
    scratch += [vm(2, *dims[1][1:]), vm(2, *dims[2][1:])]
    scratch += [vm(3, low3, wide), vm(1, low3, wide), vm(3, nyb, low3, wide), vm(1, nyb, low3, wide)]
    scratch += [vm(low3, wide), vm(low3, wide)] + [vm(nxb, low3, wide)] * 3
    where = (0, 0, 0, 1, 1, 1, 2, 2, 2)
    scratch += [vm(2, *dims[l][1:]) for l in where]
    scratch += [vm(2, dims[l][0], dims[l][2]) for l in where] * 2
    scratch += [dma(9, 4), dma(9, 4), dma(3, nyb), dma(3, nyb), dma(1, nyb), dma(1, nyb)]
    scratch += [dma(nxb)] * 4
    block = lambda l: jax.ShapeDtypeStruct((nx >> l, ny >> l, nz >> l), jnp.float32)
    whole = pl.BlockSpec(memory_space=pltpu.VMEM)
    return pl.pallas_call(
        functools.partial(kernel, nxb, nyb),
        out_shape=[block(0), block(1), block(2), block(3)],
        in_specs=[whole] * 3,
        out_specs=[whole] * 4,
        scratch_shapes=scratch,
        compiler_params=pltpu.CompilerParams(
            collective_id=0, has_side_effects=True, vmem_limit_bytes=40 * 1024 * 1024
        ),
    )(initial_guess, right_side, coefficient)


def solution(mesh):
    placed = P("xb", "yb", None)
    return jax.shard_map(
        functools.partial(per_device, mesh.shape["xb"], mesh.shape["yb"]),
        mesh=mesh,
        in_specs=(placed,) * 3,
        out_specs=(placed,) * 4,
        check_vma=False,
    )
```

```python
import functools

import jax
import jax.numpy as jnp
from jax import lax
from jax.experimental import pallas as pl
from jax.experimental.pallas import tpu as pltpu
from jax.sharding import PartitionSpec as P

COARSE_ITERS = 8
MESH = pl.DeviceIdType.MESH

damping_alpha = 0.05
cheb_theta = 1.15
cheb_delta = 0.85
cheb_sigma = cheb_theta / cheb_delta
cheb_first = 1.0 / cheb_sigma
cheb_second = 1.0 / (2.0 * cheb_sigma - cheb_first)
cheb_carry = cheb_second * cheb_first
cheb_resid = 2.0 * cheb_second / cheb_delta
jacobi_weight = 0.8

K0, V0, E0, G0, K1, E1, G1, K2, E2 = range(9)


def lane_of(shape):
    return lax.broadcasted_iota(jnp.int32, shape, 1)


def row_of(shape):
    return lax.broadcasted_iota(jnp.int32, shape, 0)


def pair_matrix(rows, columns, valid, offset=0):
    source = row_of((rows, columns))
    target = lane_of((rows, columns)) - offset
    hit = (source // 2 == target) & (source < valid) & (target >= 0)
    return jnp.where(hit, 1.0, 0.0).astype(jnp.bfloat16)


def fold_lanes(value, matrix):
    n = value.shape[0]
    high = value.astype(jnp.bfloat16)
    rest = value - high.astype(jnp.float32)
    middle = rest.astype(jnp.bfloat16)
    lowest = (rest - middle.astype(jnp.float32)).astype(jnp.bfloat16)
    if n % 16 == 0:
        parts = jnp.concatenate([high, middle, lowest], axis=0)
        out = jnp.dot(parts, matrix, preferred_element_type=jnp.float32)
        return out[0:n] + (out[n : 2 * n] + out[2 * n : 3 * n])
    out = [
        jnp.dot(p, matrix, preferred_element_type=jnp.float32) for p in (high, middle, lowest)
    ]
    return out[0] + (out[1] + out[2])


def pair_rows(value, fold):
    n = value.shape[0]
    parts = []
    for t in range(value.shape[1] // 128):
        fold[t, 0:n, :] = value[:, 128 * t : 128 * (t + 1)]
        parts.append(
            fold[t, pl.ds(0, n // 2, stride=2), :] + fold[t, pl.ds(1, n // 2, stride=2), :]
        )
    return parts[0] if len(parts) == 1 else jnp.concatenate(parts, axis=1)


class Level:
    def __init__(self, dims, valid, scale, refs):
        self.nx, self.ny, self.lanes = dims
        self.valid = valid
        self.c = 0.5 * scale
        self.wx, self.wy, self.wl, self.wz, self.al, self.di = refs

    def inner_faces(self, k):
        shape = (self.ny, self.lanes)
        lane = lane_of(shape)
        for i in range(self.nx):
            own = k(i)
            if i + 1 < self.nx:
                self.wx[i + 1] = self.c * (own + k(i + 1))
            wz = self.c * (own + pltpu.roll(own, self.lanes - 1, 1))
            self.wz[i] = jnp.where(lane < self.valid - 1, wz, 0.0)
            edge = (lane == 0) | (lane == self.valid - 1)
            self.al[i] = damping_alpha + jnp.where(edge, self.c * own, 0.0)

    def y_faces(self, k, ky):
        shape = (self.ny, self.lanes)
        row = row_of(shape)
        for i in range(self.nx):
            own = k(i)
            up = jnp.where(row == self.ny - 1, ky[1, i : i + 1, :], pltpu.roll(own, self.ny - 1, 0))
            self.wy[i] = self.c * (own + up)
            self.wl[i : i + 1, :] = self.c * (own[0:1] + ky[0, i : i + 1, :])

    def x_faces(self, k, kx):
        self.wx[0] = self.c * (k(0) + kx[0])
        self.wx[self.nx] = self.c * (k(self.nx - 1) + kx[1])

    def diagonal(self, i):
        wz, wy = self.wz[i], self.wy[i]
        row = row_of((self.ny, self.lanes))
        below = jnp.where(row == 0, self.wl[i : i + 1, :], pltpu.roll(wy, 1, 0))
        total = self.al[i] + (wz + pltpu.roll(wz, 1, 1)) + (wy + below)
        self.di[i] = 1.0 / (total + (self.wx[i] + self.wx[i + 1]))

    def operate(self, i, v, vx, vy):
        shape = (self.ny, self.lanes)
        row = row_of(shape)
        own = v(i)
        fz = self.wz[i] * (own - pltpu.roll(own, self.lanes - 1, 1))
        result = self.al[i] * own + (fz - pltpu.roll(fz, 1, 1))
        over = vy[1, i : i + 1, :] if vy is not None else 0.0
        up = jnp.where(row == self.ny - 1, over, pltpu.roll(own, self.ny - 1, 0))
        fy = self.wy[i] * (own - up)
        low = self.wl[i : i + 1, :] * ((vy[0, i : i + 1, :] if vy is not None else 0.0) - own[0:1])
        result = result + (fy - jnp.where(row == 0, low, pltpu.roll(fy, 1, 0)))
        for face, j, side in ((i, i - 1, 0), (i + 1, i + 1, 1)):
            if 0 <= j < self.nx:
                result = result + self.wx[face] * (own - v(j))
            elif vx is not None:
                result = result + self.wx[face] * (own - vx[side])
            else:
                result = result + self.wx[face] * own
        return result


def kernel(nxb, nyb, v0_hbm, f_hbm, k_hbm, *rest):
    names = []
    for l in range(3):
        fields = ("d0", "v1") if l == 0 else ("f%d" % l, "k%d" % l, "d%d" % l, "v2%d" % l)
        names += [*fields, *("%s%d" % (n, l) for n in ("wx", "wy", "wl", "wz", "al", "di", "fold"))]
    names += ["gx0", "gx1", "part", "kpart", "part_in", "kpart_in", "mine", "kmine"]
    names += ["whole", "kwhole", "last"]
    names += ["%s%d" % (n, e) for n in ("hx", "hy", "py") for e in range(9)]
    names += ["send", "recv", "psend", "precv", "kpsend", "kprecv"]
    names += ["wsend", "wrecv", "kwsend", "kwrecv", "v0", "f0", "k0", "load"]
    names += ["fine", "middle", "lower", "coarse", "store"]
    s = dict(zip(names, rest[4:], strict=True))
    held = [s[n] for n in ("fine", "middle", "lower", "coarse")]
    fine, middle, lower, coarse = held
    stores = [pltpu.make_async_copy(held[t], rest[t], s["store"].at[t]) for t in range(4)]
    hx = [s["hx%d" % e] for e in range(9)]
    hy = [s["hy%d" % e] for e in range(9)]
    py = [s["py%d" % e] for e in range(9)]
    xi, yj = lax.axis_index("xb"), lax.axis_index("yb")
    has = (xi > 0, xi < nxb - 1, yj > 0, yj < nyb - 1)
    beside = (
        (jnp.maximum(xi - 1, 0), yj),
        (jnp.minimum(xi + 1, nxb - 1), yj),
        (xi, jnp.maximum(yj - 1, 0)),
        (xi, jnp.minimum(yj + 1, nyb - 1)),
    )

    v0_ref, f_ref, k_ref = s["v0"], s["f0"], s["k0"]
    loads = [
        pltpu.make_async_copy(source, target, s["load"].at[t])
        for t, (source, target) in enumerate(((k_hbm, k_ref), (v0_hbm, v0_ref), (f_hbm, f_ref)))
    ]
    for one in loads:
        one.start()

    barrier = pltpu.get_barrier_semaphore()

    def greet(device):
        pl.semaphore_signal(barrier, inc=1, device_id=device, device_id_type=MESH)

    for o in range(1, nyb):
        greet((xi, lax.rem(yj + o, nyb)))
    for side in (0, 1):
        @pl.when(has[side])
        def _():
            for y in range(nyb):
                greet((beside[side][0], jnp.int32(y)))
    for o in range(1, nxb):
        x = lax.rem(xi + o, nxb)

        @pl.when((x - xi > 1) | (xi - x > 1))
        def _():
            greet((x, yj))
    rows = has[0].astype(jnp.int32) + has[1].astype(jnp.int32)
    pl.semaphore_wait(barrier, (nyb - 1) + nyb * rows + (nxb - 1 - rows))

    def copy(e, side, src):
        dst = (hx if side < 2 else hy)[e].at[1 - side % 2]
        return pltpu.make_async_remote_copy(
            src_ref=src,
            dst_ref=dst,
            send_sem=s["send"].at[e, side],
            recv_sem=s["recv"].at[e, side],
            device_id=beside[side],
            device_id_type=MESH,
        )

    started = []

    def put(e, side, src):
        made = copy(e, side, src)
        pl.when(has[side])(made.start)
        started.append((made, side))
        away = (hx if side < 2 else hy)[e]

        @pl.when(jnp.logical_not(has[side]))
        def _():
            away[side % 2] = jnp.zeros(away.shape[1:], jnp.float32)

    def get(e, sides):
        for side in sides:
            other = side ^ 1
            buffer = (hx if side < 2 else hy)[e]
            made = pltpu.make_async_remote_copy(
                src_ref=buffer.at[side % 2],
                dst_ref=buffer.at[side % 2],
                send_sem=s["send"].at[e, other],
                recv_sem=s["recv"].at[e, other],
                device_id=beside[other],
                device_id_type=MESH,
            )
            pl.when(has[side])(made.wait_recv)

    def put_x(e, ref):
        put(e, 0, ref.at[0])
        put(e, 1, ref.at[ref.shape[0] - 1])

    def pack(e, i, value):
        n = value.shape[0]
        py[e][0, i : i + 1, :] = value[0:1]
        py[e][1, i : i + 1, :] = value[n - 1 : n]

    def put_y(e):
        put(e, 2, py[e].at[0])
        put(e, 3, py[e].at[1])

    def restrict(planes, matrix, fold, out, start=0):
        n = planes[0].shape[0]
        pairs = [planes[2 * i] + planes[2 * i + 1] for i in range(len(planes) // 2)]
        folded = fold_lanes(jnp.concatenate(pairs, axis=0), matrix) * 0.125
        summed = pair_rows(folded, fold)
        for i in range(len(pairs)):
            out[start + i] = summed[i * (n // 2) : (i + 1) * (n // 2)]

    def gather_rows(src, into, send, recv, offsets):
        made = []
        for t, step in enumerate(offsets):
            for o in range(nyb):
                if step == 0 and o == 0:
                    continue
                y = lax.rem(yj + o, nyb)
                side = 0 if step < 0 else 1
                x = xi if step == 0 else beside[side][0]
                one = pltpu.make_async_remote_copy(
                    src_ref=src.at[t],
                    dst_ref=into.at[t, yj],
                    send_sem=send.at[t, o],
                    recv_sem=recv.at[t, yj],
                    device_id=(x, y),
                    device_id_type=MESH,
                )
                if step == 0:
                    one.start()
                else:
                    pl.when(has[side])(one.start)
                made.append((one, step))
        return made

    def gathered_rows(src, into, send, recv, offsets):
        total = src[offsets.index(0)]
        for t, step in enumerate(offsets):
            for o in range(nyb):
                if step == 0 and o == 0:
                    continue
                y = lax.rem(yj + o, nyb)
                side = 1 if step < 0 else 0
                one = pltpu.make_async_remote_copy(
                    src_ref=into.at[t, y],
                    dst_ref=into.at[t, y],
                    send_sem=send.at[t, o],
                    recv_sem=recv.at[t, y],
                    device_id=(xi, lax.rem(yj + 1, nyb)),
                    device_id_type=MESH,
                )
                if step == 0:
                    one.wait_recv()
                else:
                    pl.when(has[side])(one.wait_recv)

                    @pl.when(jnp.logical_not(has[side]))
                    def _():
                        into[t, y] = jnp.zeros(into.shape[2:], jnp.float32)
                total = total + into[t, y]
        return total

    def gather_columns(src, into, send, recv):
        made = []
        for o in range(1, nxb):
            one = pltpu.make_async_remote_copy(
                src_ref=src,
                dst_ref=into.at[xi],
                send_sem=send.at[o],
                recv_sem=recv.at[xi],
                device_id=(lax.rem(xi + o, nxb), yj),
                device_id_type=MESH,
            )
            one.start()
            made.append(one)
        return made

    def gathered_columns(src, into, send, recv):
        into[xi] = src[...]
        for o in range(1, nxb):
            x = lax.rem(xi + o, nxb)
            pltpu.make_async_remote_copy(
                src_ref=into.at[x],
                dst_ref=into.at[x],
                send_sem=send.at[o],
                recv_sem=recv.at[x],
                device_id=(lax.rem(xi + 1, nxb), yj),
                device_id_type=MESH,
            ).wait_recv()

    nx, ny, nz = k_ref.shape
    levels = []
    for l in range(3):
        dims = (nx >> l, ny >> l, max(nz >> l, 128))
        refs = [s["%s%d" % (n, l)] for n in ("wx", "wy", "wl", "wz", "al", "di")]
        levels.append(Level(dims, nz >> l, 0.25**l, refs))
    low3, nz3 = ny // 8, nz // 8
    wide = nyb * nz3
    s01 = pair_matrix(nz, max(nz // 2, 128), nz)
    s12 = pair_matrix(max(nz // 2, 128), max(nz // 4, 128), nz // 2)

    def s23(offset):
        return pair_matrix(max(nz // 4, 128), wide, nz // 4, offset * nz3)

    put_x(K0, k_hbm)
    put_x(V0, v0_hbm)
    loads[0].wait()
    for i in range(nx):
        pack(K0, i, k_ref[i])
    put_y(K0)
    loads[1].wait()
    for i in range(nx):
        pack(V0, i, v0_ref[i])
    put_y(V0)

    restrict([k_ref[i] for i in range(nx)], s01, s["fold0"], s["k1"])
    put_x(K1, s["k1"])
    for i in range(nx // 2):
        pack(K1, i, s["k1"][i])
    put_y(K1)
    restrict([s["k1"][i] for i in range(nx // 2)], s12, s["fold1"], s["k2"])
    put_x(K2, s["k2"])
    for i in range(nx // 4):
        pack(K2, i, s["k2"][i])
    put_y(K2)
    restrict([s["k2"][i] for i in range(nx // 4)], s23(yj), s["fold2"], s["kpart"])
    kargs = (s["kpart"], s["kpart_in"], s["kpsend"], s["kprecv"], (0,))
    krows = gather_rows(*kargs)

    top = levels[0]
    inner, outer = list(range(1, nx - 1)), [0, nx - 1]
    k = lambda i: k_ref[i]
    v0 = lambda i: v0_ref[i]
    d0, v1 = s["d0"], s["v1"]
    top.inner_faces(k)
    loads[2].wait()
    get(K0, (2, 3))
    get(V0, (2, 3))
    top.y_faces(k, hy[K0])

    def first(i):
        top.diagonal(i)
        r = f_ref[i] - top.operate(i, v0, hx[V0], hy[V0])
        d = r * (top.di[i] * (1.0 / cheb_theta))
        d0[i] = d
        v = v0_ref[i] + d
        v1[i] = v
        pack(E0, i, v)

    for i in inner:
        first(i)
    get(K0, (0, 1))
    get(V0, (0, 1))
    top.x_faces(k, hx[K0])
    for i in outer:
        first(i)
        put(E0, 0 if i == 0 else 1, v1.at[i])
    put_y(E0)

    s["kmine"][...] = gathered_rows(*kargs)
    kcargs = (s["kmine"], s["kwhole"], s["kwsend"], s["kwrecv"])
    kcolumns = gather_columns(*kcargs)
    for l, e, ref in ((1, K1, s["k1"]), (2, K2, s["k2"])):
        level = levels[l]
        kl = functools.partial(lambda ref, i: ref[i], ref)
        level.inner_faces(kl)
        get(e, (0, 1, 2, 3))
        level.y_faces(kl, hy[e])
        level.x_faces(kl, hx[e])
        for i in range(level.nx):
            level.diagonal(i)

    get(E0, (2, 3))

    def second(level, i, f, v1, d0, e, out):
        r = f(i) - level.operate(i, v1, hx[e], hy[e])
        v = v1(i) + (cheb_carry * d0(i) + (cheb_resid * level.di[i]) * r)
        out[i] = v
        return v

    f0 = lambda i: f_ref[i]
    v1at = lambda i: v1[i]
    d0at = lambda i: d0[i]
    def face_sums(level, out, matrix, e, gx, fold):
        n = level.ny
        both = [level.wx[0] * out[0], level.wx[level.nx] * out[level.nx - 1]]
        folded = fold_lanes(jnp.concatenate(both, axis=0), matrix) * 0.125
        summed = pair_rows(folded, fold)
        for side in (0, 1):
            gx[side] = summed[side * (n // 2) : (side + 1) * (n // 2)]
        put_x(e, gx)
        lows, highs = [], []
        for i in range(level.nx // 2):
            a, b = 2 * i, 2 * i + 1
            lows.append(level.wl[a : a + 1, :] * out[a, 0:1, :] + level.wl[b : b + 1, :] * out[b, 0:1, :])
            highs.append(
                level.wy[a, n - 1 : n, :] * out[a, n - 1 : n, :]
                + level.wy[b, n - 1 : n, :] * out[b, n - 1 : n, :]
            )
        m = level.nx // 2
        pad = [jnp.zeros((8 - m, level.lanes), jnp.float32)]
        tops = [jnp.concatenate(part + pad, axis=0) for part in (lows, highs)]
        folded = fold_lanes(jnp.concatenate(tops, axis=0), matrix) * 0.125
        py[e][0] = folded[0:m]
        py[e][1] = folded[8 : 8 + m]
        put_y(e)

    def left_over(level, f, out, pair, matrix, fold, into):
        at = lambda i: out[i]
        left = [f(i) - level.operate(i, at, None, None) for i in (2 * pair, 2 * pair + 1)]
        restrict(left, matrix, fold, into, pair)

    def next_side(level, f, out, matrix, e, gx, fold, into, done=()):
        face_sums(level, out, matrix, e, gx, fold)
        for pair in range(level.nx // 2):
            if pair not in done:
                left_over(level, f, out, pair, matrix, fold, into)
        get(e, (0, 1, 2, 3))
        m, n = level.nx // 2, level.ny // 2
        row = row_of((n, into.shape[2]))
        for i in range(m):
            value = into[i]
            if i == 0:
                value = value + hx[e][0]
            if i == m - 1:
                value = value + hx[e][1]
            value = value + jnp.where(row == 0, hy[e][0, i : i + 1, :], 0.0)
            into[i] = value + jnp.where(row == n - 1, hy[e][1, i : i + 1, :], 0.0)

    for i in inner:
        second(top, i, f0, v1at, d0at, E0, fine)
    middle_pairs = tuple(range(1, nx // 2 - 1))
    for pair in middle_pairs:
        left_over(top, f0, fine, pair, s01, s["fold0"], s["f1"])
    get(E0, (0, 1))
    for i in outer:
        second(top, i, f0, v1at, d0at, E0, fine)

    stores[0].start()
    next_side(top, f0, fine, s01, G0, s["gx0"], s["fold0"], s["f1"], middle_pairs)

    def correct(level, f, d, e, out):
        for i in range(level.nx):
            value = f[i] * (level.di[i] * (1.0 / cheb_theta))
            d[i] = value
            pack(e, i, value)
        put_x(e, d)
        put_y(e)
        get(e, (0, 1, 2, 3))
        at = lambda i: d[i]
        for i in range(level.nx):
            second(level, i, lambda i: f[i], at, at, e, out)

    correct(levels[1], s["f1"], s["d1"], E1, s["v21"])
    next_side(levels[1], lambda i: s["f1"][i], s["v21"], s12, G1, s["gx1"], s["fold1"], s["f2"])
    middle[...] = s["v21"][:, :, 0 : nz // 2]
    stores[1].start()
    low = levels[2]
    correct(low, s["f2"], s["d2"], E2, s["v22"])

    v2, f2, part = s["v22"], s["f2"], s["part"]
    n = low.ny
    left = f2[0] - low.operate(0, lambda i: v2[i], None, None)
    left = left + (f2[1] - low.operate(1, lambda i: v2[i], None, None))
    stack = [left, low.wx[0] * v2[0], low.wx[2] * v2[1]]
    folded = fold_lanes(jnp.concatenate(stack, axis=0), s23(yj)) * 0.125
    summed = pair_rows(folded, s["fold2"])
    tiles = [summed[t * (n // 2) : (t + 1) * (n // 2)] for t in range(3)]
    down = low.wl[0:1, :] * v2[0, 0:1, :] + low.wl[1:2, :] * v2[1, 0:1, :]
    up = low.wy[0, n - 1 : n, :] * v2[0, n - 1 : n, :] + low.wy[1, n - 1 : n, :] * v2[1, n - 1 : n, :]
    eight = (8, low.lanes)
    down = fold_lanes(jnp.broadcast_to(down, eight), s23(yj - 1)) * 0.125
    up = fold_lanes(jnp.broadcast_to(up, eight), s23(yj + 1)) * 0.125
    row = row_of((low3, wide))
    own = tiles[0] + jnp.where(row == low3 - 1, down[0:1], 0.0) + jnp.where(row == 0, up[0:1], 0.0)
    part[0] = tiles[1]
    part[1] = own
    part[2] = tiles[2]
    fargs = (part, s["part_in"], s["psend"], s["precv"], (-1, 0, 1))
    frows = gather_rows(*fargs)
    lower[...] = v2[:, :, 0 : nz // 4]
    stores[2].start()

    gathered_columns(*kcargs)
    shape = (nxb, wide)
    lane, xrow = lane_of(shape), row_of(shape)
    z = lax.rem(lane, nz3)
    inside = (xrow > 0, xrow < nxb - 1, z > 0, z < nz3 - 1)
    below = lane >= nz3
    above = lane < wide - nz3
    c = 0.5 * 0.25**3

    def around(v):
        first = jnp.where(below, pltpu.roll(v[-1], nz3, 1), 0.0)
        final = jnp.where(above, pltpu.roll(v[0], wide - nz3, 1), 0.0)
        out = []
        for r in range(low3):
            own = v[r]
            out.append(
                (
                    jnp.where(inside[0], pltpu.roll(own, 1, 0), 0.0),
                    jnp.where(inside[1], pltpu.roll(own, nxb - 1, 0), 0.0),
                    jnp.where(inside[2], pltpu.roll(own, 1, 1), 0.0),
                    jnp.where(inside[3], pltpu.roll(own, wide - 1, 1), 0.0),
                    v[r - 1] if r > 0 else first,
                    v[r + 1] if r < low3 - 1 else final,
                )
            )
        return out

    kc = [s["kwhole"][:, r, :] for r in range(low3)]
    weights = [[c * (kc[r] + other) for other in near] for r, near in enumerate(around(kc))]
    diagonal = [damping_alpha + sum(w) for w in weights]
    step = [jacobi_weight / d for d in diagonal]

    def operate(v):
        return [
            diagonal[r] * v[r] - sum(w * other for w, other in zip(weights[r], near))
            for r, near in enumerate(around(v))
        ]

    image = sum(operate([jnp.ones(shape, jnp.float32)] * low3))
    s["mine"][...] = gathered_rows(*fargs)
    fcargs = (s["mine"], s["whole"], s["wsend"], s["wrecv"])
    fcolumns = gather_columns(*fcargs)
    image = jnp.sum(image)
    gathered_columns(*fcargs)
    fc = [s["whole"][:, r, :] for r in range(low3)]
    v = [step[r] * fc[r] for r in range(low3)]
    for _ in range(COARSE_ITERS - 1):
        image_v = operate(v)
        v = [v[r] + step[r] * (fc[r] - image_v[r]) for r in range(low3)]
    image_v = operate(v)
    shift = jnp.sum(sum(fc[r] - image_v[r] for r in range(low3))) / image
    for r in range(low3):
        s["last"][:, r, :] = v[r] + shift
    block = s["last"][xi]
    coarse[0] = pltpu.roll(block, lax.rem(wide - yj * nz3, wide), 1)[:, 0:nz3]
    stores[3].start()

    for one in stores:
        one.wait()
    for made, side in started:
        pl.when(has[side])(made.wait_send)
    for made, step_x in krows + frows:
        if step_x == 0:
            made.wait_send()
        else:
            pl.when(has[0 if step_x < 0 else 1])(made.wait_send)
    for made in kcolumns + fcolumns:
        made.wait_send()


def write_out(*refs):
    sem = refs[8]
    copies = [pltpu.make_async_copy(refs[t], refs[4 + t], sem.at[t]) for t in range(4)]
    for one in copies:
        one.start()
    for one in copies:
        one.wait()


def per_device(nxb, nyb, initial_guess, right_side, coefficient):
    nx, ny, nz = coefficient.shape
    vm = lambda *shape: pltpu.VMEM(shape, jnp.float32)
    dma = lambda *shape: pltpu.SemaphoreType.DMA(shape)
    dims = [(nx >> l, ny >> l, max(nz >> l, 128)) for l in range(3)]
    low3, nz3 = ny // 8, nz // 8
    wide = nyb * nz3
    scratch = []
    for l, (a, b, c) in enumerate(dims):
        if l == 0:
            scratch += [vm(a, b, c), vm(a, b, c)]
        else:
            scratch += [vm(a, b, c)] * 4
        scratch += [vm(a + 1, b, c), vm(a, b, c), vm(a, c), vm(a, b, c), vm(a, b, c), vm(a, b, c)]
        folded = dims[l + 1][2] if l < 2 else wide
        scratch += [vm(folded // 128, max(a // 2, 3) * b + 8, 128)]
    scratch += [vm(2, *dims[1][1:]), vm(2, *dims[2][1:])]
    scratch += [vm(3, low3, wide), vm(1, low3, wide), vm(3, nyb, low3, wide), vm(1, nyb, low3, wide)]
    scratch += [vm(low3, wide), vm(low3, wide)] + [vm(nxb, low3, wide)] * 3
    where = (0, 0, 0, 1, 1, 1, 2, 2, 2)
    scratch += [vm(2, *dims[l][1:]) for l in where]
    scratch += [vm(2, dims[l][0], dims[l][2]) for l in where] * 2
    scratch += [dma(9, 4), dma(9, 4), dma(3, nyb), dma(3, nyb), dma(1, nyb), dma(1, nyb)]
    scratch += [dma(nxb)] * 4
    scratch += [vm(nx, ny, nz)] * 3 + [dma(3)]
    scratch += [vm(nx >> l, ny >> l, nz >> l) for l in range(4)] + [dma(4)]
    block = lambda l: jax.ShapeDtypeStruct((nx >> l, ny >> l, nz >> l), jnp.float32)
    anywhere = pl.BlockSpec(memory_space=pl.ANY)
    fields = pl.pallas_call(
        functools.partial(kernel, nxb, nyb),
        out_shape=[block(0), block(1), block(2), block(3)],
        in_specs=[anywhere] * 3,
        out_specs=[anywhere] * 4,
        scratch_shapes=scratch,
        compiler_params=pltpu.CompilerParams(
            collective_id=0, has_side_effects=True, vmem_limit_bytes=56 * 1024 * 1024
        ),
    )(initial_guess, right_side, coefficient)
    return pl.pallas_call(
        write_out,
        out_shape=[block(0), block(1), block(2), block(3)],
        in_specs=[anywhere] * 4,
        out_specs=[anywhere] * 4,
        scratch_shapes=[dma(4)],
        compiler_params=pltpu.CompilerParams(vmem_limit_bytes=56 * 1024 * 1024),
    )(*fields)


def solution(mesh):
    placed = P("xb", "yb", None)
    return jax.shard_map(
        functools.partial(per_device, mesh.shape["xb"], mesh.shape["yb"]),
        mesh=mesh,
        in_specs=(placed,) * 3,
        out_specs=(placed,) * 4,
        check_vma=False,
    )
```

```python
import functools

import jax
import jax.numpy as jnp
from jax import lax
from jax.experimental import pallas as pl
from jax.experimental.pallas import tpu as pltpu
from jax.sharding import PartitionSpec as P

COARSE_ITERS = 8
MESH = pl.DeviceIdType.MESH

damping_alpha = 0.05
cheb_theta = 1.15
cheb_delta = 0.85
cheb_sigma = cheb_theta / cheb_delta
cheb_first = 1.0 / cheb_sigma
cheb_second = 1.0 / (2.0 * cheb_sigma - cheb_first)
cheb_carry = cheb_second * cheb_first
cheb_resid = 2.0 * cheb_second / cheb_delta
jacobi_weight = 0.8

K0, V0, E0, G0, K1, E1, G1, K2, E2 = range(9)


def lane_of(shape):
    return lax.broadcasted_iota(jnp.int32, shape, 1)


def row_of(shape):
    return lax.broadcasted_iota(jnp.int32, shape, 0)


def pair_matrix(rows, columns, valid, offset=0):
    source = row_of((rows, columns))
    target = lane_of((rows, columns)) - offset
    hit = (source // 2 == target) & (source < valid) & (target >= 0)
    return jnp.where(hit, 1.0, 0.0).astype(jnp.bfloat16)


def fold_lanes(value, matrix):
    n = value.shape[0]
    high = value.astype(jnp.bfloat16)
    rest = value - high.astype(jnp.float32)
    middle = rest.astype(jnp.bfloat16)
    lowest = (rest - middle.astype(jnp.float32)).astype(jnp.bfloat16)
    if n % 16 == 0:
        parts = jnp.concatenate([high, middle, lowest], axis=0)
        out = jnp.dot(parts, matrix, preferred_element_type=jnp.float32)
        return out[0:n] + (out[n : 2 * n] + out[2 * n : 3 * n])
    out = [
        jnp.dot(p, matrix, preferred_element_type=jnp.float32) for p in (high, middle, lowest)
    ]
    return out[0] + (out[1] + out[2])


def pair_rows(value, fold):
    n = value.shape[0]
    parts = []
    for t in range(value.shape[1] // 128):
        fold[t, 0:n, :] = value[:, 128 * t : 128 * (t + 1)]
        parts.append(
            fold[t, pl.ds(0, n // 2, stride=2), :] + fold[t, pl.ds(1, n // 2, stride=2), :]
        )
    return parts[0] if len(parts) == 1 else jnp.concatenate(parts, axis=1)


class Level:
    def __init__(self, dims, valid, scale, refs):
        self.nx, self.ny, self.lanes = dims
        self.valid = valid
        self.c = 0.5 * scale
        self.wx, self.wy, self.wl, self.wz, self.al, self.di = refs

    def planes(self, body):
        if self.nx > 4:
            pl.loop(0, self.nx)(body)
        else:
            for i in range(self.nx):
                body(i)

    def inner_faces(self, k):
        shape = (self.ny, self.lanes)
        lane = lane_of(shape)
        for i in range(self.nx - 1) if self.nx <= 4 else ():
            self.wx[i + 1] = self.c * (k(i) + k(i + 1))
        if self.nx > 4:
            @pl.loop(0, self.nx - 1)
            def _(i):
                self.wx[i + 1] = self.c * (k(i) + k(i + 1))

        def body(i):
            own = k(i)
            wz = self.c * (own + pltpu.roll(own, self.lanes - 1, 1))
            self.wz[i] = jnp.where(lane < self.valid - 1, wz, 0.0)
            edge = (lane == 0) | (lane == self.valid - 1)
            self.al[i] = damping_alpha + jnp.where(edge, self.c * own, 0.0)

        self.planes(body)

    def y_faces(self, k, ky):
        shape = (self.ny, self.lanes)
        row = row_of(shape)

        def body(i):
            own = k(i)
            up = jnp.where(row == self.ny - 1, ky[1, pl.ds(i, 1), :], pltpu.roll(own, self.ny - 1, 0))
            self.wy[i] = self.c * (own + up)
            self.wl[pl.ds(i, 1), :] = self.c * (own[0:1] + ky[0, pl.ds(i, 1), :])

        self.planes(body)

    def x_faces(self, k, kx):
        self.wx[0] = self.c * (k(0) + kx[0])
        self.wx[self.nx] = self.c * (k(self.nx - 1) + kx[1])

    def diagonal(self, i):
        wz, wy = self.wz[i], self.wy[i]
        row = row_of((self.ny, self.lanes))
        below = jnp.where(row == 0, self.wl[pl.ds(i, 1), :], pltpu.roll(wy, 1, 0))
        total = self.al[i] + (wz + pltpu.roll(wz, 1, 1)) + (wy + below)
        self.di[i] = 1.0 / (total + (self.wx[i] + self.wx[i + 1]))

    def operate(self, i, v, vx, vy):
        shape = (self.ny, self.lanes)
        row = row_of(shape)
        own = v(i)
        fz = self.wz[i] * (own - pltpu.roll(own, self.lanes - 1, 1))
        result = self.al[i] * own + (fz - pltpu.roll(fz, 1, 1))
        over = vy[1, pl.ds(i, 1), :] if vy is not None else 0.0
        up = jnp.where(row == self.ny - 1, over, pltpu.roll(own, self.ny - 1, 0))
        fy = self.wy[i] * (own - up)
        low = self.wl[pl.ds(i, 1), :] * ((vy[0, pl.ds(i, 1), :] if vy is not None else 0.0) - own[0:1])
        result = result + (fy - jnp.where(row == 0, low, pltpu.roll(fy, 1, 0)))
        for face, j, side in ((i, i - 1, 0), (i + 1, i + 1, 1)):
            if not isinstance(i, int) or 0 <= j < self.nx:
                result = result + self.wx[face] * (own - v(j))
            elif vx is not None:
                result = result + self.wx[face] * (own - vx[side])
            else:
                result = result + self.wx[face] * own
        return result


def kernel(nxb, nyb, v0_hbm, f_hbm, k_hbm, *rest):
    names = []
    for l in range(3):
        fields = ("d0", "v1") if l == 0 else ("f%d" % l, "k%d" % l, "d%d" % l, "v2%d" % l)
        names += [*fields, *("%s%d" % (n, l) for n in ("wx", "wy", "wl", "wz", "al", "di", "fold"))]
    names += ["gx0", "gx1", "part", "kpart", "part_in", "kpart_in", "mine", "kmine"]
    names += ["whole", "kwhole", "last"]
    names += ["%s%d" % (n, e) for n in ("hx", "hy", "py") for e in range(9)]
    names += ["send", "recv", "psend", "precv", "kpsend", "kprecv"]
    names += ["wsend", "wrecv", "kwsend", "kwrecv", "v0", "f0", "k0", "load"]
    names += ["fine", "middle", "lower", "coarse", "store"]
    s = dict(zip(names, rest[4:], strict=True))
    held = [s[n] for n in ("fine", "middle", "lower", "coarse")]
    fine, middle, lower, coarse = held
    stores = [pltpu.make_async_copy(held[t], rest[t], s["store"].at[t]) for t in range(4)]
    hx = [s["hx%d" % e] for e in range(9)]
    hy = [s["hy%d" % e] for e in range(9)]
    py = [s["py%d" % e] for e in range(9)]
    xi, yj = lax.axis_index("xb"), lax.axis_index("yb")
    has = (xi > 0, xi < nxb - 1, yj > 0, yj < nyb - 1)
    beside = (
        (jnp.maximum(xi - 1, 0), yj),
        (jnp.minimum(xi + 1, nxb - 1), yj),
        (xi, jnp.maximum(yj - 1, 0)),
        (xi, jnp.minimum(yj + 1, nyb - 1)),
    )

    v0_ref, f_ref, k_ref = s["v0"], s["f0"], s["k0"]
    loads = [
        pltpu.make_async_copy(source, target, s["load"].at[t])
        for t, (source, target) in enumerate(((k_hbm, k_ref), (v0_hbm, v0_ref), (f_hbm, f_ref)))
    ]
    for one in loads:
        one.start()

    barrier = pltpu.get_barrier_semaphore()

    def greet(device):
        pl.semaphore_signal(barrier, inc=1, device_id=device, device_id_type=MESH)

    for o in range(1, nyb):
        greet((xi, lax.rem(yj + o, nyb)))
    for side in (0, 1):
        @pl.when(has[side])
        def _():
            for y in range(nyb):
                greet((beside[side][0], jnp.int32(y)))
    for o in range(1, nxb):
        x = lax.rem(xi + o, nxb)

        @pl.when((x - xi > 1) | (xi - x > 1))
        def _():
            greet((x, yj))
    rows = has[0].astype(jnp.int32) + has[1].astype(jnp.int32)
    pl.semaphore_wait(barrier, (nyb - 1) + nyb * rows + (nxb - 1 - rows))

    def copy(e, side, src):
        dst = (hx if side < 2 else hy)[e].at[1 - side % 2]
        return pltpu.make_async_remote_copy(
            src_ref=src,
            dst_ref=dst,
            send_sem=s["send"].at[e, side],
            recv_sem=s["recv"].at[e, side],
            device_id=beside[side],
            device_id_type=MESH,
        )

    started = []

    def put(e, side, src):
        made = copy(e, side, src)
        pl.when(has[side])(made.start)
        started.append((made, side))
        away = (hx if side < 2 else hy)[e]

        @pl.when(jnp.logical_not(has[side]))
        def _():
            away[side % 2] = jnp.zeros(away.shape[1:], jnp.float32)

    def get(e, sides):
        for side in sides:
            other = side ^ 1
            buffer = (hx if side < 2 else hy)[e]
            made = pltpu.make_async_remote_copy(
                src_ref=buffer.at[side % 2],
                dst_ref=buffer.at[side % 2],
                send_sem=s["send"].at[e, other],
                recv_sem=s["recv"].at[e, other],
                device_id=beside[other],
                device_id_type=MESH,
            )
            pl.when(has[side])(made.wait_recv)

    def put_x(e, ref):
        put(e, 0, ref.at[0])
        put(e, 1, ref.at[ref.shape[0] - 1])

    def pack(e, i, value):
        n = value.shape[0]
        py[e][0, pl.ds(i, 1), :] = value[0:1]
        py[e][1, pl.ds(i, 1), :] = value[n - 1 : n]

    def put_y(e):
        put(e, 2, py[e].at[0])
        put(e, 3, py[e].at[1])

    def restrict(planes, matrix, fold, out, start=0):
        n = planes[0].shape[0]
        pairs = [planes[2 * i] + planes[2 * i + 1] for i in range(len(planes) // 2)]
        folded = fold_lanes(jnp.concatenate(pairs, axis=0), matrix) * 0.125
        summed = pair_rows(folded, fold)
        for i in range(len(pairs)):
            out[start + i] = summed[i * (n // 2) : (i + 1) * (n // 2)]

    def gather_rows(src, into, send, recv, offsets):
        made = []
        for t, step in enumerate(offsets):
            for o in range(nyb):
                if step == 0 and o == 0:
                    continue
                y = lax.rem(yj + o, nyb)
                side = 0 if step < 0 else 1
                x = xi if step == 0 else beside[side][0]
                one = pltpu.make_async_remote_copy(
                    src_ref=src.at[t],
                    dst_ref=into.at[t, yj],
                    send_sem=send.at[t, o],
                    recv_sem=recv.at[t, yj],
                    device_id=(x, y),
                    device_id_type=MESH,
                )
                if step == 0:
                    one.start()
                else:
                    pl.when(has[side])(one.start)
                made.append((one, step))
        return made

    def gathered_rows(src, into, send, recv, offsets):
        total = src[offsets.index(0)]
        for t, step in enumerate(offsets):
            for o in range(nyb):
                if step == 0 and o == 0:
                    continue
                y = lax.rem(yj + o, nyb)
                side = 1 if step < 0 else 0
                one = pltpu.make_async_remote_copy(
                    src_ref=into.at[t, y],
                    dst_ref=into.at[t, y],
                    send_sem=send.at[t, o],
                    recv_sem=recv.at[t, y],
                    device_id=(xi, lax.rem(yj + 1, nyb)),
                    device_id_type=MESH,
                )
                if step == 0:
                    one.wait_recv()
                else:
                    pl.when(has[side])(one.wait_recv)

                    @pl.when(jnp.logical_not(has[side]))
                    def _():
                        into[t, y] = jnp.zeros(into.shape[2:], jnp.float32)
                total = total + into[t, y]
        return total

    def gather_columns(src, into, send, recv):
        made = []
        for o in range(1, nxb):
            one = pltpu.make_async_remote_copy(
                src_ref=src,
                dst_ref=into.at[xi],
                send_sem=send.at[o],
                recv_sem=recv.at[xi],
                device_id=(lax.rem(xi + o, nxb), yj),
                device_id_type=MESH,
            )
            one.start()
            made.append(one)
        return made

    def gathered_columns(src, into, send, recv):
        into[xi] = src[...]
        for o in range(1, nxb):
            x = lax.rem(xi + o, nxb)
            pltpu.make_async_remote_copy(
                src_ref=into.at[x],
                dst_ref=into.at[x],
                send_sem=send.at[o],
                recv_sem=recv.at[x],
                device_id=(lax.rem(xi + 1, nxb), yj),
                device_id_type=MESH,
            ).wait_recv()

    nx, ny, nz = k_ref.shape
    levels = []
    for l in range(3):
        dims = (nx >> l, ny >> l, max(nz >> l, 128))
        refs = [s["%s%d" % (n, l)] for n in ("wx", "wy", "wl", "wz", "al", "di")]
        levels.append(Level(dims, nz >> l, 0.25**l, refs))
    low3, nz3 = ny // 8, nz // 8
    wide = nyb * nz3
    s01 = pair_matrix(nz, max(nz // 2, 128), nz)
    s12 = pair_matrix(max(nz // 2, 128), max(nz // 4, 128), nz // 2)

    def s23(offset):
        return pair_matrix(max(nz // 4, 128), wide, nz // 4, offset * nz3)

    put_x(K0, k_hbm)
    put_x(V0, v0_hbm)
    loads[0].wait()
    for i in range(nx):
        pack(K0, i, k_ref[i])
    put_y(K0)
    loads[1].wait()
    for i in range(nx):
        pack(V0, i, v0_ref[i])
    put_y(V0)

    restrict([k_ref[i] for i in range(nx)], s01, s["fold0"], s["k1"])
    put_x(K1, s["k1"])
    for i in range(nx // 2):
        pack(K1, i, s["k1"][i])
    put_y(K1)
    restrict([s["k1"][i] for i in range(nx // 2)], s12, s["fold1"], s["k2"])
    put_x(K2, s["k2"])
    for i in range(nx // 4):
        pack(K2, i, s["k2"][i])
    put_y(K2)
    restrict([s["k2"][i] for i in range(nx // 4)], s23(yj), s["fold2"], s["kpart"])
    kargs = (s["kpart"], s["kpart_in"], s["kpsend"], s["kprecv"], (0,))
    krows = gather_rows(*kargs)

    top = levels[0]
    outer = [0, nx - 1]
    k = lambda i: k_ref[i]
    v0 = lambda i: v0_ref[i]
    d0, v1 = s["d0"], s["v1"]
    top.inner_faces(k)
    loads[2].wait()
    get(K0, (2, 3))
    get(V0, (2, 3))
    top.y_faces(k, hy[K0])

    def first(i):
        top.diagonal(i)
        r = f_ref[i] - top.operate(i, v0, hx[V0], hy[V0])
        d = r * (top.di[i] * (1.0 / cheb_theta))
        d0[i] = d
        v = v0_ref[i] + d
        v1[i] = v
        pack(E0, i, v)

    pl.loop(1, nx - 1)(first)
    get(K0, (0, 1))
    get(V0, (0, 1))
    top.x_faces(k, hx[K0])
    for i in outer:
        first(i)
        put(E0, 0 if i == 0 else 1, v1.at[i])
    put_y(E0)

    s["kmine"][...] = gathered_rows(*kargs)
    kcargs = (s["kmine"], s["kwhole"], s["kwsend"], s["kwrecv"])
    kcolumns = gather_columns(*kcargs)
    for l, e, ref in ((1, K1, s["k1"]), (2, K2, s["k2"])):
        level = levels[l]
        kl = functools.partial(lambda ref, i: ref[i], ref)
        level.inner_faces(kl)
        get(e, (0, 1, 2, 3))
        level.y_faces(kl, hy[e])
        level.x_faces(kl, hx[e])
        for i in range(level.nx):
            level.diagonal(i)

    get(E0, (2, 3))

    def second(level, i, f, v1, d0, e, out):
        r = f(i) - level.operate(i, v1, hx[e], hy[e])
        v = v1(i) + (cheb_carry * d0(i) + (cheb_resid * level.di[i]) * r)
        out[i] = v
        return v

    f0 = lambda i: f_ref[i]
    v1at = lambda i: v1[i]
    d0at = lambda i: d0[i]
    def face_sums(level, out, matrix, e, gx, fold):
        n = level.ny
        both = [level.wx[0] * out[0], level.wx[level.nx] * out[level.nx - 1]]
        folded = fold_lanes(jnp.concatenate(both, axis=0), matrix) * 0.125
        summed = pair_rows(folded, fold)
        for side in (0, 1):
            gx[side] = summed[side * (n // 2) : (side + 1) * (n // 2)]
        put_x(e, gx)
        lows, highs = [], []
        for i in range(level.nx // 2):
            a, b = 2 * i, 2 * i + 1
            lows.append(level.wl[a : a + 1, :] * out[a, 0:1, :] + level.wl[b : b + 1, :] * out[b, 0:1, :])
            highs.append(
                level.wy[a, n - 1 : n, :] * out[a, n - 1 : n, :]
                + level.wy[b, n - 1 : n, :] * out[b, n - 1 : n, :]
            )
        m = level.nx // 2
        pad = [jnp.zeros((8 - m, level.lanes), jnp.float32)]
        tops = [jnp.concatenate(part + pad, axis=0) for part in (lows, highs)]
        folded = fold_lanes(jnp.concatenate(tops, axis=0), matrix) * 0.125
        py[e][0] = folded[0:m]
        py[e][1] = folded[8 : 8 + m]
        put_y(e)

    def left_over(level, f, out, pair, matrix, fold, into):
        at = lambda i: out[i]
        left = [f(i) - level.operate(i, at, None, None) for i in (2 * pair, 2 * pair + 1)]
        restrict(left, matrix, fold, into, pair)

    def next_side(level, f, out, matrix, e, gx, fold, into, done=()):
        face_sums(level, out, matrix, e, gx, fold)
        for pair in range(level.nx // 2):
            if pair not in done:
                left_over(level, f, out, pair, matrix, fold, into)
        get(e, (0, 1, 2, 3))
        m, n = level.nx // 2, level.ny // 2
        row = row_of((n, into.shape[2]))
        for i in range(m):
            value = into[i]
            if i == 0:
                value = value + hx[e][0]
            if i == m - 1:
                value = value + hx[e][1]
            value = value + jnp.where(row == 0, hy[e][0, i : i + 1, :], 0.0)
            into[i] = value + jnp.where(row == n - 1, hy[e][1, i : i + 1, :], 0.0)

    @pl.loop(1, nx - 1)
    def _(i):
        second(top, i, f0, v1at, d0at, E0, fine)

    middle_pairs = tuple(range(1, nx // 2 - 1))

    @pl.loop(1, nx // 2 - 1)
    def _(pair):
        left_over(top, f0, fine, pair, s01, s["fold0"], s["f1"])

    get(E0, (0, 1))
    for i in outer:
        second(top, i, f0, v1at, d0at, E0, fine)

    stores[0].start()
    next_side(top, f0, fine, s01, G0, s["gx0"], s["fold0"], s["f1"], middle_pairs)

    def correct(level, f, d, e, out):
        for i in range(level.nx):
            value = f[i] * (level.di[i] * (1.0 / cheb_theta))
            d[i] = value
            pack(e, i, value)
        put_x(e, d)
        put_y(e)
        get(e, (0, 1, 2, 3))
        at = lambda i: d[i]
        for i in range(level.nx):
            second(level, i, lambda i: f[i], at, at, e, out)

    correct(levels[1], s["f1"], s["d1"], E1, s["v21"])
    next_side(levels[1], lambda i: s["f1"][i], s["v21"], s12, G1, s["gx1"], s["fold1"], s["f2"])
    middle[...] = s["v21"][:, :, 0 : nz // 2]
    stores[1].start()
    low = levels[2]
    correct(low, s["f2"], s["d2"], E2, s["v22"])

    v2, f2, part = s["v22"], s["f2"], s["part"]
    n = low.ny
    left = f2[0] - low.operate(0, lambda i: v2[i], None, None)
    left = left + (f2[1] - low.operate(1, lambda i: v2[i], None, None))
    stack = [left, low.wx[0] * v2[0], low.wx[2] * v2[1]]
    folded = fold_lanes(jnp.concatenate(stack, axis=0), s23(yj)) * 0.125
    summed = pair_rows(folded, s["fold2"])
    tiles = [summed[t * (n // 2) : (t + 1) * (n // 2)] for t in range(3)]
    down = low.wl[0:1, :] * v2[0, 0:1, :] + low.wl[1:2, :] * v2[1, 0:1, :]
    up = low.wy[0, n - 1 : n, :] * v2[0, n - 1 : n, :] + low.wy[1, n - 1 : n, :] * v2[1, n - 1 : n, :]
    eight = (8, low.lanes)
    down = fold_lanes(jnp.broadcast_to(down, eight), s23(yj - 1)) * 0.125
    up = fold_lanes(jnp.broadcast_to(up, eight), s23(yj + 1)) * 0.125
    row = row_of((low3, wide))
    own = tiles[0] + jnp.where(row == low3 - 1, down[0:1], 0.0) + jnp.where(row == 0, up[0:1], 0.0)
    part[0] = tiles[1]
    part[1] = own
    part[2] = tiles[2]
    fargs = (part, s["part_in"], s["psend"], s["precv"], (-1, 0, 1))
    frows = gather_rows(*fargs)
    lower[...] = v2[:, :, 0 : nz // 4]
    stores[2].start()

    gathered_columns(*kcargs)
    shape = (nxb, wide)
    lane, xrow = lane_of(shape), row_of(shape)
    z = lax.rem(lane, nz3)
    inside = (xrow > 0, xrow < nxb - 1, z > 0, z < nz3 - 1)
    below = lane >= nz3
    above = lane < wide - nz3
    c = 0.5 * 0.25**3

    def around(v):
        first = jnp.where(below, pltpu.roll(v[-1], nz3, 1), 0.0)
        final = jnp.where(above, pltpu.roll(v[0], wide - nz3, 1), 0.0)
        out = []
        for r in range(low3):
            own = v[r]
            out.append(
                (
                    jnp.where(inside[0], pltpu.roll(own, 1, 0), 0.0),
                    jnp.where(inside[1], pltpu.roll(own, nxb - 1, 0), 0.0),
                    jnp.where(inside[2], pltpu.roll(own, 1, 1), 0.0),
                    jnp.where(inside[3], pltpu.roll(own, wide - 1, 1), 0.0),
                    v[r - 1] if r > 0 else first,
                    v[r + 1] if r < low3 - 1 else final,
                )
            )
        return out

    kc = [s["kwhole"][:, r, :] for r in range(low3)]
    weights = [[c * (kc[r] + other) for other in near] for r, near in enumerate(around(kc))]
    diagonal = [damping_alpha + sum(w) for w in weights]
    step = [jacobi_weight / d for d in diagonal]

    def operate(v):
        return [
            diagonal[r] * v[r] - sum(w * other for w, other in zip(weights[r], near))
            for r, near in enumerate(around(v))
        ]

    image = sum(operate([jnp.ones(shape, jnp.float32)] * low3))
    s["mine"][...] = gathered_rows(*fargs)
    fcargs = (s["mine"], s["whole"], s["wsend"], s["wrecv"])
    fcolumns = gather_columns(*fcargs)
    image = jnp.sum(image)
    gathered_columns(*fcargs)
    fc = [s["whole"][:, r, :] for r in range(low3)]
    v = [step[r] * fc[r] for r in range(low3)]
    for _ in range(COARSE_ITERS - 1):
        image_v = operate(v)
        v = [v[r] + step[r] * (fc[r] - image_v[r]) for r in range(low3)]
    image_v = operate(v)
    shift = jnp.sum(sum(fc[r] - image_v[r] for r in range(low3))) / image
    for r in range(low3):
        s["last"][:, r, :] = v[r] + shift
    block = s["last"][xi]
    coarse[0] = pltpu.roll(block, lax.rem(wide - yj * nz3, wide), 1)[:, 0:nz3]
    stores[3].start()

    for one in stores:
        one.wait()
    for made, side in started:
        pl.when(has[side])(made.wait_send)
    for made, step_x in krows + frows:
        if step_x == 0:
            made.wait_send()
        else:
            pl.when(has[0 if step_x < 0 else 1])(made.wait_send)
    for made in kcolumns + fcolumns:
        made.wait_send()


def write_out(*refs):
    sources, targets, held, into, out = refs[0:4], refs[4:8], refs[8:12], refs[12], refs[13]
    pieces = []
    for t in range(4):
        for i in range(sources[t].shape[0]):
            pieces.append((sources[t].at[i], held[t].at[i], targets[t].at[i]))
    loads = [pltpu.make_async_copy(a, b, into.at[j]) for j, (a, b, _) in enumerate(pieces)]
    stores = [pltpu.make_async_copy(b, c, out.at[j]) for j, (_, b, c) in enumerate(pieces)]
    for one in loads:
        one.start()
    for load, store in zip(loads, stores):
        load.wait()
        store.start()
    for one in stores:
        one.wait()


def per_device(nxb, nyb, initial_guess, right_side, coefficient):
    nx, ny, nz = coefficient.shape
    vm = lambda *shape: pltpu.VMEM(shape, jnp.float32)
    dma = lambda *shape: pltpu.SemaphoreType.DMA(shape)
    dims = [(nx >> l, ny >> l, max(nz >> l, 128)) for l in range(3)]
    low3, nz3 = ny // 8, nz // 8
    wide = nyb * nz3
    scratch = []
    for l, (a, b, c) in enumerate(dims):
        if l == 0:
            scratch += [vm(a, b, c), vm(a, b, c)]
        else:
            scratch += [vm(a, b, c)] * 4
        scratch += [vm(a + 1, b, c), vm(a, b, c), vm(a, c), vm(a, b, c), vm(a, b, c), vm(a, b, c)]
        folded = dims[l + 1][2] if l < 2 else wide
        scratch += [vm(folded // 128, max(a // 2, 3) * b + 8, 128)]
    scratch += [vm(2, *dims[1][1:]), vm(2, *dims[2][1:])]
    scratch += [vm(3, low3, wide), vm(1, low3, wide), vm(3, nyb, low3, wide), vm(1, nyb, low3, wide)]
    scratch += [vm(low3, wide), vm(low3, wide)] + [vm(nxb, low3, wide)] * 3
    where = (0, 0, 0, 1, 1, 1, 2, 2, 2)
    scratch += [vm(2, *dims[l][1:]) for l in where]
    scratch += [vm(2, dims[l][0], dims[l][2]) for l in where] * 2
    scratch += [dma(9, 4), dma(9, 4), dma(3, nyb), dma(3, nyb), dma(1, nyb), dma(1, nyb)]
    scratch += [dma(nxb)] * 4
    scratch += [vm(nx, ny, nz)] * 3 + [dma(3)]
    scratch += [vm(nx >> l, ny >> l, nz >> l) for l in range(4)] + [dma(4)]
    block = lambda l: jax.ShapeDtypeStruct((nx >> l, ny >> l, nz >> l), jnp.float32)
    anywhere = pl.BlockSpec(memory_space=pl.ANY)
    fields = pl.pallas_call(
        functools.partial(kernel, nxb, nyb),
        out_shape=[block(0), block(1), block(2), block(3)],
        in_specs=[anywhere] * 3,
        out_specs=[anywhere] * 4,
        scratch_shapes=scratch,
        compiler_params=pltpu.CompilerParams(
            collective_id=0, has_side_effects=True, vmem_limit_bytes=56 * 1024 * 1024
        ),
    )(initial_guess, right_side, coefficient)
    return pl.pallas_call(
        write_out,
        out_shape=[block(0), block(1), block(2), block(3)],
        in_specs=[anywhere] * 4,
        out_specs=[anywhere] * 4,
        scratch_shapes=[vm(nx >> l, ny >> l, nz >> l) for l in range(4)]
        + [dma(sum(nx >> l for l in range(4)))] * 2,
        compiler_params=pltpu.CompilerParams(vmem_limit_bytes=56 * 1024 * 1024),
    )(*fields)


def solution(mesh):
    placed = P("xb", "yb", None)
    return jax.shard_map(
        functools.partial(per_device, mesh.shape["xb"], mesh.shape["yb"]),
        mesh=mesh,
        in_specs=(placed,) * 3,
        out_specs=(placed,) * 4,
        check_vma=False,
    )
```

```python
import functools

import jax
import jax.numpy as jnp
from jax import lax
from jax.experimental import pallas as pl
from jax.experimental.pallas import tpu as pltpu
from jax.sharding import PartitionSpec as P

COARSE_ITERS = 8
MESH = pl.DeviceIdType.MESH

damping_alpha = 0.05
cheb_theta = 1.15
cheb_delta = 0.85
cheb_sigma = cheb_theta / cheb_delta
cheb_first = 1.0 / cheb_sigma
cheb_second = 1.0 / (2.0 * cheb_sigma - cheb_first)
cheb_carry = cheb_second * cheb_first
cheb_resid = 2.0 * cheb_second / cheb_delta
jacobi_weight = 0.8

K0, V0, E0, G0, K1, E1, G1, K2, E2 = range(9)


def lane_of(shape):
    return lax.broadcasted_iota(jnp.int32, shape, 1)


def row_of(shape):
    return lax.broadcasted_iota(jnp.int32, shape, 0)


def pair_matrix(rows, columns, valid, offset=0):
    source = row_of((rows, columns))
    target = lane_of((rows, columns)) - offset
    hit = (source // 2 == target) & (source < valid) & (target >= 0)
    return jnp.where(hit, 1.0, 0.0).astype(jnp.bfloat16)


def fold_lanes(value, matrix):
    n = value.shape[0]
    high = value.astype(jnp.bfloat16)
    rest = value - high.astype(jnp.float32)
    middle = rest.astype(jnp.bfloat16)
    lowest = (rest - middle.astype(jnp.float32)).astype(jnp.bfloat16)
    if n % 16 == 0:
        parts = jnp.concatenate([high, middle, lowest], axis=0)
        out = jnp.dot(parts, matrix, preferred_element_type=jnp.float32)
        return out[0:n] + (out[n : 2 * n] + out[2 * n : 3 * n])
    out = [
        jnp.dot(p, matrix, preferred_element_type=jnp.float32) for p in (high, middle, lowest)
    ]
    return out[0] + (out[1] + out[2])


def pair_rows(value, fold):
    n = value.shape[0]
    parts = []
    for t in range(value.shape[1] // 128):
        fold[t, 0:n, :] = value[:, 128 * t : 128 * (t + 1)]
        parts.append(
            fold[t, pl.ds(0, n // 2, stride=2), :] + fold[t, pl.ds(1, n // 2, stride=2), :]
        )
    return parts[0] if len(parts) == 1 else jnp.concatenate(parts, axis=1)


class Level:
    def __init__(self, dims, valid, scale, refs):
        self.nx, self.ny, self.lanes = dims
        self.valid = valid
        self.c = 0.5 * scale
        self.wx, self.wy, self.wl, self.wz, self.al, self.di = refs

    def planes(self, body):
        if self.nx > 4:
            pl.loop(0, self.nx)(body)
        else:
            for i in range(self.nx):
                body(i)

    def inner_faces(self, k):
        shape = (self.ny, self.lanes)
        lane = lane_of(shape)
        for i in range(self.nx - 1) if self.nx <= 4 else ():
            self.wx[i + 1] = self.c * (k(i) + k(i + 1))
        if self.nx > 4:
            @pl.loop(0, self.nx - 1)
            def _(i):
                self.wx[i + 1] = self.c * (k(i) + k(i + 1))

        def body(i):
            own = k(i)
            wz = self.c * (own + pltpu.roll(own, self.lanes - 1, 1))
            self.wz[i] = jnp.where(lane < self.valid - 1, wz, 0.0)
            edge = (lane == 0) | (lane == self.valid - 1)
            self.al[i] = damping_alpha + jnp.where(edge, self.c * own, 0.0)

        self.planes(body)

    def y_faces(self, k, ky):
        shape = (self.ny, self.lanes)
        row = row_of(shape)

        def body(i):
            own = k(i)
            up = jnp.where(row == self.ny - 1, ky[1, pl.ds(i, 1), :], pltpu.roll(own, self.ny - 1, 0))
            self.wy[i] = self.c * (own + up)
            self.wl[pl.ds(i, 1), :] = self.c * (own[0:1] + ky[0, pl.ds(i, 1), :])

        self.planes(body)

    def x_faces(self, k, kx):
        self.wx[0] = self.c * (k(0) + kx[0])
        self.wx[self.nx] = self.c * (k(self.nx - 1) + kx[1])

    def diagonal(self, i):
        wz, wy = self.wz[i], self.wy[i]
        row = row_of((self.ny, self.lanes))
        below = jnp.where(row == 0, self.wl[pl.ds(i, 1), :], pltpu.roll(wy, 1, 0))
        total = self.al[i] + (wz + pltpu.roll(wz, 1, 1)) + (wy + below)
        self.di[i] = 1.0 / (total + (self.wx[i] + self.wx[i + 1]))

    def operate(self, i, v, vx, vy):
        shape = (self.ny, self.lanes)
        row = row_of(shape)
        own = v(i)
        fz = self.wz[i] * (own - pltpu.roll(own, self.lanes - 1, 1))
        result = self.al[i] * own + (fz - pltpu.roll(fz, 1, 1))
        over = vy[1, pl.ds(i, 1), :] if vy is not None else 0.0
        up = jnp.where(row == self.ny - 1, over, pltpu.roll(own, self.ny - 1, 0))
        fy = self.wy[i] * (own - up)
        low = self.wl[pl.ds(i, 1), :] * ((vy[0, pl.ds(i, 1), :] if vy is not None else 0.0) - own[0:1])
        result = result + (fy - jnp.where(row == 0, low, pltpu.roll(fy, 1, 0)))
        for face, j, side in ((i, i - 1, 0), (i + 1, i + 1, 1)):
            if not isinstance(i, int) or 0 <= j < self.nx:
                result = result + self.wx[face] * (own - v(j))
            elif vx is not None:
                result = result + self.wx[face] * (own - vx[side])
            else:
                result = result + self.wx[face] * own
        return result


def kernel(nxb, nyb, v0_hbm, f_hbm, k_hbm, *rest):
    names = []
    for l in range(3):
        fields = ("d0", "v1") if l == 0 else ("f%d" % l, "k%d" % l, "d%d" % l, "v2%d" % l)
        names += [*fields, *("%s%d" % (n, l) for n in ("wx", "wy", "wl", "wz", "al", "di", "fold"))]
    names += ["gx0", "gx1", "part", "kpart", "part_in", "kpart_in", "mine", "kmine"]
    names += ["whole", "kwhole", "last"]
    names += ["%s%d" % (n, e) for n in ("hx", "hy", "py") for e in range(9)]
    names += ["send", "recv", "psend", "precv", "kpsend", "kprecv"]
    names += ["wsend", "wrecv", "kwsend", "kwrecv", "v0", "f0", "k0", "load"]
    names += ["fine", "middle", "lower", "coarse", "store"]
    s = dict(zip(names, rest[4:], strict=True))
    held = [s[n] for n in ("fine", "middle", "lower", "coarse")]
    fine, middle, lower, coarse = held
    stores = [pltpu.make_async_copy(held[t], rest[t], s["store"].at[t]) for t in range(4)]
    hx = [s["hx%d" % e] for e in range(9)]
    hy = [s["hy%d" % e] for e in range(9)]
    py = [s["py%d" % e] for e in range(9)]
    xi, yj = lax.axis_index("xb"), lax.axis_index("yb")
    has = (xi > 0, xi < nxb - 1, yj > 0, yj < nyb - 1)
    beside = (
        (jnp.maximum(xi - 1, 0), yj),
        (jnp.minimum(xi + 1, nxb - 1), yj),
        (xi, jnp.maximum(yj - 1, 0)),
        (xi, jnp.minimum(yj + 1, nyb - 1)),
    )

    v0_ref, f_ref, k_ref = s["v0"], s["f0"], s["k0"]
    loads = [
        pltpu.make_async_copy(source, target, s["load"].at[t])
        for t, (source, target) in enumerate(((k_hbm, k_ref), (v0_hbm, v0_ref), (f_hbm, f_ref)))
    ]
    for one in loads:
        one.start()

    barrier = pltpu.get_barrier_semaphore()

    def greet(device):
        pl.semaphore_signal(barrier, inc=1, device_id=device, device_id_type=MESH)

    for o in range(1, nyb):
        greet((xi, lax.rem(yj + o, nyb)))
    for side in (0, 1):
        @pl.when(has[side])
        def _():
            for y in range(nyb):
                greet((beside[side][0], jnp.int32(y)))
    for o in range(1, nxb):
        x = lax.rem(xi + o, nxb)

        @pl.when((x - xi > 1) | (xi - x > 1))
        def _():
            greet((x, yj))
    rows = has[0].astype(jnp.int32) + has[1].astype(jnp.int32)
    pl.semaphore_wait(barrier, (nyb - 1) + nyb * rows + (nxb - 1 - rows))

    def copy(e, side, src):
        dst = (hx if side < 2 else hy)[e].at[1 - side % 2]
        return pltpu.make_async_remote_copy(
            src_ref=src,
            dst_ref=dst,
            send_sem=s["send"].at[e, side],
            recv_sem=s["recv"].at[e, side],
            device_id=beside[side],
            device_id_type=MESH,
        )

    started = []

    def put(e, side, src):
        made = copy(e, side, src)
        pl.when(has[side])(made.start)
        started.append((made, side))

    def get(e, sides):
        for side in sides:
            other = side ^ 1
            buffer = (hx if side < 2 else hy)[e]
            made = pltpu.make_async_remote_copy(
                src_ref=buffer.at[side % 2],
                dst_ref=buffer.at[side % 2],
                send_sem=s["send"].at[e, other],
                recv_sem=s["recv"].at[e, other],
                device_id=beside[other],
                device_id_type=MESH,
            )
            pl.when(has[side])(made.wait_recv)

    def put_x(e, ref):
        put(e, 0, ref.at[0])
        put(e, 1, ref.at[ref.shape[0] - 1])

    def pack(e, i, value):
        n = value.shape[0]
        py[e][0, pl.ds(i, 1), :] = value[0:1]
        py[e][1, pl.ds(i, 1), :] = value[n - 1 : n]

    def put_y(e):
        put(e, 2, py[e].at[0])
        put(e, 3, py[e].at[1])

    def restrict(planes, matrix, fold, out, start=0):
        n = planes[0].shape[0]
        pairs = [planes[2 * i] + planes[2 * i + 1] for i in range(len(planes) // 2)]
        folded = fold_lanes(jnp.concatenate(pairs, axis=0), matrix) * 0.125
        summed = pair_rows(folded, fold)
        for i in range(len(pairs)):
            out[start + i] = summed[i * (n // 2) : (i + 1) * (n // 2)]

    def gather_rows(src, into, send, recv, offsets):
        made = []
        for t, step in enumerate(offsets):
            for o in range(nyb):
                if step == 0 and o == 0:
                    continue
                y = lax.rem(yj + o, nyb)
                side = 0 if step < 0 else 1
                x = xi if step == 0 else beside[side][0]
                one = pltpu.make_async_remote_copy(
                    src_ref=src.at[t],
                    dst_ref=into.at[t, yj],
                    send_sem=send.at[t, o],
                    recv_sem=recv.at[t, yj],
                    device_id=(x, y),
                    device_id_type=MESH,
                )
                if step == 0:
                    one.start()
                else:
                    pl.when(has[side])(one.start)
                made.append((one, step))
        return made

    def gathered_rows(src, into, send, recv, offsets):
        total = src[offsets.index(0)]
        for t, step in enumerate(offsets):
            for o in range(nyb):
                if step == 0 and o == 0:
                    continue
                y = lax.rem(yj + o, nyb)
                side = 1 if step < 0 else 0
                one = pltpu.make_async_remote_copy(
                    src_ref=into.at[t, y],
                    dst_ref=into.at[t, y],
                    send_sem=send.at[t, o],
                    recv_sem=recv.at[t, y],
                    device_id=(xi, lax.rem(yj + 1, nyb)),
                    device_id_type=MESH,
                )
                if step == 0:
                    one.wait_recv()
                else:
                    pl.when(has[side])(one.wait_recv)

                    @pl.when(jnp.logical_not(has[side]))
                    def _():
                        into[t, y] = jnp.zeros(into.shape[2:], jnp.float32)
                total = total + into[t, y]
        return total

    def gather_columns(src, into, send, recv):
        made = []
        for o in range(1, nxb):
            one = pltpu.make_async_remote_copy(
                src_ref=src,
                dst_ref=into.at[xi],
                send_sem=send.at[o],
                recv_sem=recv.at[xi],
                device_id=(lax.rem(xi + o, nxb), yj),
                device_id_type=MESH,
            )
            one.start()
            made.append(one)
        return made

    def gathered_columns(src, into, send, recv):
        into[xi] = src[...]
        for o in range(1, nxb):
            x = lax.rem(xi + o, nxb)
            pltpu.make_async_remote_copy(
                src_ref=into.at[x],
                dst_ref=into.at[x],
                send_sem=send.at[o],
                recv_sem=recv.at[x],
                device_id=(lax.rem(xi + 1, nxb), yj),
                device_id_type=MESH,
            ).wait_recv()

    nx, ny, nz = k_ref.shape
    levels = []
    for l in range(3):
        dims = (nx >> l, ny >> l, max(nz >> l, 128))
        refs = [s["%s%d" % (n, l)] for n in ("wx", "wy", "wl", "wz", "al", "di")]
        levels.append(Level(dims, nz >> l, 0.25**l, refs))
    low3, nz3 = ny // 8, nz // 8
    wide = nyb * nz3
    s01 = pair_matrix(nz, max(nz // 2, 128), nz)
    s12 = pair_matrix(max(nz // 2, 128), max(nz // 4, 128), nz // 2)

    def s23(offset):
        return pair_matrix(max(nz // 4, 128), wide, nz // 4, offset * nz3)

    put_x(K0, k_hbm)
    put_x(V0, v0_hbm)
    loads[0].wait()
    for i in range(nx):
        pack(K0, i, k_ref[i])
    put_y(K0)
    loads[1].wait()
    for i in range(nx):
        pack(V0, i, v0_ref[i])
    put_y(V0)
    for side in range(4):
        @pl.when(jnp.logical_not(has[side]))
        def _():
            for away in hx if side < 2 else hy:
                away[side % 2] = jnp.zeros(away.shape[1:], jnp.float32)

    restrict([k_ref[i] for i in range(nx)], s01, s["fold0"], s["k1"])
    put_x(K1, s["k1"])
    for i in range(nx // 2):
        pack(K1, i, s["k1"][i])
    put_y(K1)
    restrict([s["k1"][i] for i in range(nx // 2)], s12, s["fold1"], s["k2"])
    put_x(K2, s["k2"])
    for i in range(nx // 4):
        pack(K2, i, s["k2"][i])
    put_y(K2)
    restrict([s["k2"][i] for i in range(nx // 4)], s23(yj), s["fold2"], s["kpart"])
    kargs = (s["kpart"], s["kpart_in"], s["kpsend"], s["kprecv"], (0,))
    krows = gather_rows(*kargs)

    top = levels[0]
    outer = [0, nx - 1]
    k = lambda i: k_ref[i]
    v0 = lambda i: v0_ref[i]
    d0, v1 = s["d0"], s["v1"]
    top.inner_faces(k)
    loads[2].wait()
    get(K0, (2, 3))
    get(V0, (2, 3))
    top.y_faces(k, hy[K0])

    def first(i):
        top.diagonal(i)
        r = f_ref[i] - top.operate(i, v0, hx[V0], hy[V0])
        d = r * (top.di[i] * (1.0 / cheb_theta))
        d0[i] = d
        v = v0_ref[i] + d
        v1[i] = v
        pack(E0, i, v)

    pl.loop(1, nx - 1)(first)
    get(K0, (0, 1))
    get(V0, (0, 1))
    top.x_faces(k, hx[K0])
    for i in outer:
        first(i)
        put(E0, 0 if i == 0 else 1, v1.at[i])
    put_y(E0)

    s["kmine"][...] = gathered_rows(*kargs)
    kcargs = (s["kmine"], s["kwhole"], s["kwsend"], s["kwrecv"])
    kcolumns = gather_columns(*kcargs)
    for l, e, ref in ((1, K1, s["k1"]), (2, K2, s["k2"])):
        level = levels[l]
        kl = functools.partial(lambda ref, i: ref[i], ref)
        level.inner_faces(kl)
        get(e, (0, 1, 2, 3))
        level.y_faces(kl, hy[e])
        level.x_faces(kl, hx[e])
        for i in range(level.nx):
            level.diagonal(i)

    get(E0, (2, 3))

    def second(level, i, f, v1, d0, e, out):
        r = f(i) - level.operate(i, v1, hx[e], hy[e])
        v = v1(i) + (cheb_carry * d0(i) + (cheb_resid * level.di[i]) * r)
        out[i] = v
        return v

    f0 = lambda i: f_ref[i]
    v1at = lambda i: v1[i]
    d0at = lambda i: d0[i]
    def face_sums(level, out, matrix, e, gx, fold):
        n = level.ny
        both = [level.wx[0] * out[0], level.wx[level.nx] * out[level.nx - 1]]
        folded = fold_lanes(jnp.concatenate(both, axis=0), matrix) * 0.125
        summed = pair_rows(folded, fold)
        for side in (0, 1):
            gx[side] = summed[side * (n // 2) : (side + 1) * (n // 2)]
        put_x(e, gx)
        lows, highs = [], []
        for i in range(level.nx // 2):
            a, b = 2 * i, 2 * i + 1
            lows.append(level.wl[a : a + 1, :] * out[a, 0:1, :] + level.wl[b : b + 1, :] * out[b, 0:1, :])
            highs.append(
                level.wy[a, n - 1 : n, :] * out[a, n - 1 : n, :]
                + level.wy[b, n - 1 : n, :] * out[b, n - 1 : n, :]
            )
        m = level.nx // 2
        pad = [jnp.zeros((8 - m, level.lanes), jnp.float32)]
        tops = [jnp.concatenate(part + pad, axis=0) for part in (lows, highs)]
        folded = fold_lanes(jnp.concatenate(tops, axis=0), matrix) * 0.125
        py[e][0] = folded[0:m]
        py[e][1] = folded[8 : 8 + m]
        put_y(e)

    def left_over(level, f, out, pair, matrix, fold, into):
        at = lambda i: out[i]
        left = [f(i) - level.operate(i, at, None, None) for i in (2 * pair, 2 * pair + 1)]
        restrict(left, matrix, fold, into, pair)

    def next_side(level, f, out, matrix, e, gx, fold, into, done=()):
        face_sums(level, out, matrix, e, gx, fold)
        for pair in range(level.nx // 2):
            if pair not in done:
                left_over(level, f, out, pair, matrix, fold, into)
        get(e, (0, 1, 2, 3))
        m, n = level.nx // 2, level.ny // 2
        row = row_of((n, into.shape[2]))
        for i in range(m):
            value = into[i]
            if i == 0:
                value = value + hx[e][0]
            if i == m - 1:
                value = value + hx[e][1]
            value = value + jnp.where(row == 0, hy[e][0, i : i + 1, :], 0.0)
            into[i] = value + jnp.where(row == n - 1, hy[e][1, i : i + 1, :], 0.0)

    @pl.loop(1, nx - 1)
    def _(i):
        second(top, i, f0, v1at, d0at, E0, fine)

    middle_pairs = tuple(range(1, nx // 2 - 1))

    @pl.loop(1, nx // 2 - 1)
    def _(pair):
        left_over(top, f0, fine, pair, s01, s["fold0"], s["f1"])

    get(E0, (0, 1))
    for i in outer:
        second(top, i, f0, v1at, d0at, E0, fine)

    stores[0].start()
    next_side(top, f0, fine, s01, G0, s["gx0"], s["fold0"], s["f1"], middle_pairs)

    def correct(level, f, d, e, out):
        for i in range(level.nx):
            value = f[i] * (level.di[i] * (1.0 / cheb_theta))
            d[i] = value
            pack(e, i, value)
        put_x(e, d)
        put_y(e)
        get(e, (0, 1, 2, 3))
        at = lambda i: d[i]
        for i in range(level.nx):
            second(level, i, lambda i: f[i], at, at, e, out)

    correct(levels[1], s["f1"], s["d1"], E1, s["v21"])
    next_side(levels[1], lambda i: s["f1"][i], s["v21"], s12, G1, s["gx1"], s["fold1"], s["f2"])
    middle[...] = s["v21"][:, :, 0 : nz // 2]
    stores[1].start()
    low = levels[2]
    correct(low, s["f2"], s["d2"], E2, s["v22"])

    v2, f2, part = s["v22"], s["f2"], s["part"]
    n = low.ny
    left = f2[0] - low.operate(0, lambda i: v2[i], None, None)
    left = left + (f2[1] - low.operate(1, lambda i: v2[i], None, None))
    stack = [left, low.wx[0] * v2[0], low.wx[2] * v2[1]]
    folded = fold_lanes(jnp.concatenate(stack, axis=0), s23(yj)) * 0.125
    summed = pair_rows(folded, s["fold2"])
    tiles = [summed[t * (n // 2) : (t + 1) * (n // 2)] for t in range(3)]
    down = low.wl[0:1, :] * v2[0, 0:1, :] + low.wl[1:2, :] * v2[1, 0:1, :]
    up = low.wy[0, n - 1 : n, :] * v2[0, n - 1 : n, :] + low.wy[1, n - 1 : n, :] * v2[1, n - 1 : n, :]
    eight = (8, low.lanes)
    down = fold_lanes(jnp.broadcast_to(down, eight), s23(yj - 1)) * 0.125
    up = fold_lanes(jnp.broadcast_to(up, eight), s23(yj + 1)) * 0.125
    row = row_of((low3, wide))
    own = tiles[0] + jnp.where(row == low3 - 1, down[0:1], 0.0) + jnp.where(row == 0, up[0:1], 0.0)
    part[0] = tiles[1]
    part[1] = own
    part[2] = tiles[2]
    fargs = (part, s["part_in"], s["psend"], s["precv"], (-1, 0, 1))
    frows = gather_rows(*fargs)
    lower[...] = v2[:, :, 0 : nz // 4]
    stores[2].start()

    gathered_columns(*kcargs)
    shape = (nxb, wide)
    lane, xrow = lane_of(shape), row_of(shape)
    z = lax.rem(lane, nz3)
    inside = (xrow > 0, xrow < nxb - 1, z > 0, z < nz3 - 1)
    below = lane >= nz3
    above = lane < wide - nz3
    c = 0.5 * 0.25**3

    def around(v):
        first = jnp.where(below, pltpu.roll(v[-1], nz3, 1), 0.0)
        final = jnp.where(above, pltpu.roll(v[0], wide - nz3, 1), 0.0)
        out = []
        for r in range(low3):
            own = v[r]
            out.append(
                (
                    jnp.where(inside[0], pltpu.roll(own, 1, 0), 0.0),
                    jnp.where(inside[1], pltpu.roll(own, nxb - 1, 0), 0.0),
                    jnp.where(inside[2], pltpu.roll(own, 1, 1), 0.0),
                    jnp.where(inside[3], pltpu.roll(own, wide - 1, 1), 0.0),
                    v[r - 1] if r > 0 else first,
                    v[r + 1] if r < low3 - 1 else final,
                )
            )
        return out

    kc = [s["kwhole"][:, r, :] for r in range(low3)]
    weights = [[c * (kc[r] + other) for other in near] for r, near in enumerate(around(kc))]
    diagonal = [damping_alpha + sum(w) for w in weights]
    step = [jacobi_weight / d for d in diagonal]

    def operate(v):
        return [
            diagonal[r] * v[r] - sum(w * other for w, other in zip(weights[r], near))
            for r, near in enumerate(around(v))
        ]

    image = sum(operate([jnp.ones(shape, jnp.float32)] * low3))

    def left(rows):
        for made, step_x in rows:
            if step_x == 0:
                made.wait_send()
            else:
                pl.when(has[0 if step_x < 0 else 1])(made.wait_send)

    for side in range(4):
        @pl.when(has[side])
        def _():
            for made, toward in started:
                if toward == side:
                    made.wait_send()
    left(krows)
    for made in kcolumns:
        made.wait_send()
    s["mine"][...] = gathered_rows(*fargs)
    fcargs = (s["mine"], s["whole"], s["wsend"], s["wrecv"])
    fcolumns = gather_columns(*fcargs)
    image = jnp.sum(image)
    left(frows)
    gathered_columns(*fcargs)
    fc = [s["whole"][:, r, :] for r in range(low3)]
    v = [step[r] * fc[r] for r in range(low3)]
    for _ in range(COARSE_ITERS - 1):
        image_v = operate(v)
        v = [v[r] + step[r] * (fc[r] - image_v[r]) for r in range(low3)]
    image_v = operate(v)
    shift = jnp.sum(sum(fc[r] - image_v[r] for r in range(low3))) / image
    for r in range(low3):
        s["last"][:, r, :] = v[r] + shift
    block = s["last"][xi]
    coarse[0] = pltpu.roll(block, lax.rem(wide - yj * nz3, wide), 1)[:, 0:nz3]
    stores[3].start()

    for one in stores:
        one.wait()
    for made in fcolumns:
        made.wait_send()


def write_out(*refs):
    sources, targets, held, into, out = refs[0:4], refs[4:8], refs[8:12], refs[12], refs[13]
    pieces = []
    for t in range(4):
        for i in range(sources[t].shape[0]):
            pieces.append((sources[t].at[i], held[t].at[i], targets[t].at[i]))
    loads = [pltpu.make_async_copy(a, b, into.at[j]) for j, (a, b, _) in enumerate(pieces)]
    stores = [pltpu.make_async_copy(b, c, out.at[j]) for j, (_, b, c) in enumerate(pieces)]
    for one in loads:
        one.start()
    for load, store in zip(loads, stores):
        load.wait()
        store.start()
    for one in stores:
        one.wait()


def per_device(nxb, nyb, initial_guess, right_side, coefficient):
    nx, ny, nz = coefficient.shape
    vm = lambda *shape: pltpu.VMEM(shape, jnp.float32)
    dma = lambda *shape: pltpu.SemaphoreType.DMA(shape)
    dims = [(nx >> l, ny >> l, max(nz >> l, 128)) for l in range(3)]
    low3, nz3 = ny // 8, nz // 8
    wide = nyb * nz3
    scratch = []
    for l, (a, b, c) in enumerate(dims):
        if l == 0:
            scratch += [vm(a, b, c), vm(a, b, c)]
        else:
            scratch += [vm(a, b, c)] * 4
        scratch += [vm(a + 1, b, c), vm(a, b, c), vm(a, c), vm(a, b, c), vm(a, b, c), vm(a, b, c)]
        folded = dims[l + 1][2] if l < 2 else wide
        scratch += [vm(folded // 128, max(a // 2, 3) * b + 8, 128)]
    scratch += [vm(2, *dims[1][1:]), vm(2, *dims[2][1:])]
    scratch += [vm(3, low3, wide), vm(1, low3, wide), vm(3, nyb, low3, wide), vm(1, nyb, low3, wide)]
    scratch += [vm(low3, wide), vm(low3, wide)] + [vm(nxb, low3, wide)] * 3
    where = (0, 0, 0, 1, 1, 1, 2, 2, 2)
    scratch += [vm(2, *dims[l][1:]) for l in where]
    scratch += [vm(2, dims[l][0], dims[l][2]) for l in where] * 2
    scratch += [dma(9, 4), dma(9, 4), dma(3, nyb), dma(3, nyb), dma(1, nyb), dma(1, nyb)]
    scratch += [dma(nxb)] * 4
    scratch += [vm(nx, ny, nz)] * 3 + [dma(3)]
    scratch += [vm(nx >> l, ny >> l, nz >> l) for l in range(4)] + [dma(4)]
    block = lambda l: jax.ShapeDtypeStruct((nx >> l, ny >> l, nz >> l), jnp.float32)
    anywhere = pl.BlockSpec(memory_space=pl.ANY)
    fields = pl.pallas_call(
        functools.partial(kernel, nxb, nyb),
        out_shape=[block(0), block(1), block(2), block(3)],
        in_specs=[anywhere] * 3,
        out_specs=[anywhere] * 4,
        scratch_shapes=scratch,
        compiler_params=pltpu.CompilerParams(
            collective_id=0, has_side_effects=True, vmem_limit_bytes=56 * 1024 * 1024
        ),
    )(initial_guess, right_side, coefficient)
    return pl.pallas_call(
        write_out,
        out_shape=[block(0), block(1), block(2), block(3)],
        in_specs=[anywhere] * 4,
        out_specs=[anywhere] * 4,
        scratch_shapes=[vm(nx >> l, ny >> l, nz >> l) for l in range(4)]
        + [dma(sum(nx >> l for l in range(4)))] * 2,
        compiler_params=pltpu.CompilerParams(vmem_limit_bytes=56 * 1024 * 1024),
    )(*fields)


def solution(mesh):
    placed = P("xb", "yb", None)
    return jax.shard_map(
        functools.partial(per_device, mesh.shape["xb"], mesh.shape["yb"]),
        mesh=mesh,
        in_specs=(placed,) * 3,
        out_specs=(placed,) * 4,
        check_vma=False,
    )
```
